32 devices in a mesh: fsdp: 16 (over z, y, core), tp: 2 (over x).
Axes of the slice: x: 2, y: 2, z: 4, core: 2. Of those that a mesh axis runs over, the one named last changes fastest.
Arguments:
- tokens: bfloat16 [16384, 1024], P(('fsdp', 'tp')), may hold values from -6 to 6
- segments: int32 [16384], P('fsdp'), may hold values from 0 to 2, as said below
- slots: int32 [16, 32, 256], P('fsdp', 'tp'), may hold values from -1 to 1023, as said below
- gate_values: float32 [16, 32, 256], P('fsdp', 'tp'), may hold values from 0.1 to 0.5
- gains: float32 [2, 1024], P(None, ('fsdp', 'tp')), may hold values from 0.5 to 1.5
- w_query: bfloat16 [1024, 1024], P('fsdp', 'tp'), may hold values from -0.1875 to 0.1875
- w_key: bfloat16 [1024, 512], P('fsdp', 'tp'), may hold values from -0.1875 to 0.1875
- w_value: bfloat16 [1024, 512], P('fsdp', 'tp'), may hold values from -0.1875 to 0.1875
- w_out: bfloat16 [1024, 1024], P('fsdp', 'tp'), may hold values from -2 to 2
- w_gate: bfloat16 [1024, 16384], P('fsdp', 'tp'), may hold values from -0.1875 to 0.1875
- w_up: bfloat16 [1024, 16384], P('fsdp', 'tp'), may hold values from -0.1875 to 0.1875
- w_down: bfloat16 [1024, 16384], P('fsdp', 'tp'), may hold values from -0.25 to 0.25
- cotangent: bfloat16 [16384, 1024], P(('fsdp', 'tp')), may hold values from -6 to 6
Outputs:
- mixed: bfloat16 [16384, 1024], P(('fsdp', 'tp'))
- grad_tokens: float32 [16384, 1024], P(('fsdp', 'tp'))
- grad_gains: float32 [2, 1024], P(None, ('fsdp', 'tp'))
- grad_query: float32 [1024, 1024], P('fsdp', 'tp')
- grad_key: float32 [1024, 512], P('fsdp', 'tp')
- grad_value: float32 [1024, 512], P('fsdp', 'tp')
- grad_out: float32 [1024, 1024], P('fsdp', 'tp')
- grad_gate: float32 [1024, 16384], P('fsdp', 'tp')
- grad_up: float32 [1024, 16384], P('fsdp', 'tp')
- grad_down: float32 [1024, 16384], P('fsdp', 'tp')
The draws below stay inside these ranges and needn't reach their ends.
Inputs may be any that keep to these rules, and one draw needn't show every extreme that they name: `segments`: ids count documents within each packed sequence of 1024 tokens and never fall along it; every packed sequence holds documents 0, 1 and 2, the first ending within its first 512 tokens and the last starting within its last 512 tokens. `slots`: entries are token positions within the packed sequence; -1 marks an empty slot. A token stands at most once in a block and in at most 8 blocks of its sequence; the live entries of a block increase along it; in every packed sequence some expert's block has no empty slot.
All inputs are finite; a program needn't handle non-finite values.
Results may differ from the reference program's by a relative error of at most 0.018.
Values may be sent and summed in bfloat16 or wider, within the bound.
No kernel may reach another device: no remote copies, remote signals or barrier semaphores. Data moves between devices by JAX's collectives and lax.ppermute only.
A program may use at most 320 MiB of HBM per device.

```python
import jax
import jax.numpy as jnp
from jax import lax

D = 1024
Q_HEADS = 16
KV_HEADS = 8
HEAD_DIM = 64
EXPERTS = 32
FF = 512
TOP = 8
TOK_DEV = 1024
ROWS = 512
CAP = 256
GROUPS = 16
TOKENS = 16384


def draw_segments(key, part):
    key = jax.random.fold_in(key, 11)
    first_key, second_key = jax.random.split(key)
    first_cut = jax.random.randint(first_key, (GROUPS, 1), 1, ROWS)
    last_cut = jax.random.randint(second_key, (GROUPS, 1), TOK_DEV - ROWS + 1, TOK_DEV)
    positions = jnp.arange(TOK_DEV, dtype=jnp.int32)[None, :]
    doc_ids = (positions >= first_cut).astype(jnp.int32) + (positions >= last_cut).astype(jnp.int32)
    return doc_ids.reshape(TOKENS)


def slot_table(key):
    perm_key, pick_key, drop_key, full_key = jax.random.split(key, 4)
    placed_at = jax.random.permutation(perm_key, TOK_DEV).astype(jnp.int32)
    residue = placed_at % EXPERTS
    bucket = placed_at // EXPERTS
    rank_keys = jax.random.randint(pick_key, (TOK_DEV // EXPERTS, EXPERTS), 0, 1 << 20) * EXPERTS + jnp.arange(EXPERTS, dtype=jnp.int32)[None, :]
    offsets = jnp.argsort(rank_keys, axis=1, stable=True)[:, :TOP].astype(jnp.int32)
    chosen = (residue[:, None] + offsets[bucket]) % EXPERTS
    flat_chosen = chosen.reshape(-1)
    order_keys = flat_chosen * (TOK_DEV * TOP) + jnp.arange(TOK_DEV * TOP, dtype=jnp.int32)
    ordering = jnp.argsort(order_keys, stable=True).astype(jnp.int32)
    token_of = (ordering // TOP).reshape(EXPERTS, CAP)
    dropped = jax.random.randint(drop_key, (EXPERTS, CAP), 0, 8) == 0
    full_expert = jax.random.randint(full_key, (), 0, EXPERTS)
    dropped = dropped & (jnp.arange(EXPERTS, dtype=jnp.int32)[:, None] != full_expert)
    return jnp.where(dropped, -1, token_of).astype(jnp.int32)


def draw_slots(key, part):
    key = jax.random.fold_in(key, 5)
    return jax.vmap(slot_table)(jax.random.split(key, GROUPS))


def with_spikes(array, key, source, target, shards_of, factor):
    owner, partner = [(jnp.arange(array.shape[axis_at]) // (array.shape[axis_at] // shards_of)).reshape([-1 if axis == axis_at else 1 for axis in range(array.ndim)]) for axis_at in (source, target)]
    chosen = jax.random.permutation(key, shards_of)[partner]
    strong = (owner == chosen) | (owner == (partner + shards_of // 2) % shards_of)
    return jnp.where(strong, factor * array, array)


def steps_of(stream_key, dims, pieces, smallest, high):
    def one(dim, blocks):
        draws = jax.random.uniform(jax.random.fold_in(jax.random.fold_in(stream_key, 6), dim), (blocks,), jnp.float32, smallest / len(pieces), high / len(pieces))
        return jnp.repeat(jnp.exp(draws), dims[dim] // blocks).reshape((-1,) + (1,) * (len(dims) - dim - 1))

    factor_of = one(*pieces[0])
    for cut in pieces[1:]:
        factor_of = factor_of * one(*cut)
    return factor_of


def bell_draw(key, dims, width, bound, pieces=(), kind=jnp.bfloat16):
    values = width * jax.random.normal(key, dims, jnp.float32)
    if pieces:
        values = values * steps_of(key, dims, pieces, -0.22, 0.18)
    return jnp.clip(values, -bound, bound).astype(kind)


def noise_with(rng, shape, scale, most, cuts, heavy, held_as=jnp.bfloat16):
    array = scale * jax.random.normal(rng, shape, jnp.float32)
    if cuts:
        array = array * steps_of(rng, shape, cuts, -0.22, 0.18)
    return jnp.clip(with_spikes(array, jax.random.fold_in(rng, 3), *heavy), -most, most).astype(held_as)


def setup_inputs(seed: int = 0) -> dict:
    key_list = jax.random.split(jax.random.key(seed), 14)
    return {
        "tokens": noise_with(key_list[0], (TOKENS, D), 1.0, 6.0, ((0, 32),), (0, 1, 32, 2.75)),
        "segments": draw_segments(jax.random.fold_in(key_list[13], 71), 0),
        "slots": draw_slots(jax.random.fold_in(key_list[13], 71), 0),
        "gate_values": jnp.clip(0.1 + 0.4 * jax.random.uniform(key_list[3], (GROUPS, EXPERTS, CAP), jnp.float32) ** steps_of(key_list[3], (GROUPS, EXPERTS, CAP), ((0, 16), (1, 2)), -0.2, 0.2), 0.1, 0.5),
        "gains": jnp.clip(1.0 + 0.1 * jax.random.normal(key_list[4], (2, D), jnp.float32), 0.5, 1.5),
        "w_query": bell_draw(key_list[5], (D, Q_HEADS * HEAD_DIM), D ** -0.5, 0.1875, ((0, 16), (1, 2))),
        "w_key": bell_draw(key_list[6], (D, KV_HEADS * HEAD_DIM), D ** -0.5, 0.1875, ((0, 16), (1, 2))),
        "w_value": bell_draw(key_list[7], (D, KV_HEADS * HEAD_DIM), D ** -0.5, 0.1875, ((0, 16), (1, 2))),
        "w_out": bell_draw(key_list[8], (D, Q_HEADS * HEAD_DIM), 8 ** -0.5, 2.0, ((0, 16), (1, 2))),
        "w_gate": bell_draw(key_list[9], (D, EXPERTS * FF), D ** -0.5, 0.1875, ((0, 16), (1, 2))),
        "w_up": bell_draw(key_list[10], (D, EXPERTS * FF), D ** -0.5, 0.1875, ((0, 16), (1, 2))),
        "w_down": bell_draw(key_list[11], (D, EXPERTS * FF), FF ** -0.5, 0.25, ((0, 16), (1, 2))),
        "cotangent": noise_with(key_list[12], (TOKENS, D), 1.0, 6.0, ((0, 32),), (0, 1, 32, 2.75)),
    }


EPS = 1e-06

@jax.custom_vjp
def low(v):
    return lax.optimization_barrier(v.astype(jnp.bfloat16)).astype(jnp.float32)

@jax.custom_vjp
def low_back(v):
    return v

def low_keep(v):
    return (low(v), None)

def low_pass(kept, grad):
    return (grad,)

def back_keep(v):
    return (v, None)

def back_low(kept, grad):
    return (low(grad),)
low.defvjp(low_keep, low_pass)
low_back.defvjp(back_keep, back_low)

def norm_apply(values, gain_row):
    return values * lax.rsqrt(lax.optimization_barrier(jnp.mean(values * values, axis=-1, keepdims=True)) + EPS) * gain_row

def sequence_layer(resid, seg_ids, slot_index, slot_gates, gain_rows, query_w, key_w, value_w, out_w, gate_w, up_w, down_w):
    highest = lax.Precision.HIGHEST
    seq_length = resid.shape[0]
    group_size = Q_HEADS // KV_HEADS
    first_low = low(norm_apply(resid, gain_rows[0]))
    queries = low_back(low(jnp.dot(first_low, query_w, precision=highest)))
    keys_all = low_back(low(jnp.dot(first_low, key_w, precision=highest)))
    values_all = low_back(low(jnp.dot(first_low, value_w, precision=highest)))
    query_heads = queries.reshape(seq_length, KV_HEADS, group_size, HEAD_DIM)
    key_heads = keys_all.reshape(seq_length, KV_HEADS, HEAD_DIM)
    value_heads = values_all.reshape(seq_length, KV_HEADS, HEAD_DIM)
    scores = low_back(jnp.einsum('qkgd,tkd->kgqt', query_heads, key_heads, precision=highest) * HEAD_DIM ** (-0.5))
    positions = jnp.arange(seq_length, dtype=jnp.int32)
    allowed = (positions[:, None] >= positions[None, :]) & (seg_ids[:, None] == seg_ids[None, :])
    scores = jnp.where(allowed, scores, -1e+30)
    probabilities = jax.nn.softmax(scores, axis=-1)
    attended = jnp.einsum('kgqt,tkd->qkgd', low(probabilities), value_heads, precision=highest)
    attended = low_back(low(attended)).reshape(seq_length, Q_HEADS * HEAD_DIM)
    attn_out = low_back(lax.dot_general(attended, out_w, (((1,), (1,)), ((), ())), precision=highest))
    hidden = resid + attn_out
    second_low = low(norm_apply(hidden, gain_rows[1]))
    live_slot = slot_index >= 0
    safe_index = jnp.where(live_slot, slot_index, 0).astype(jnp.int32)
    slot_weight = jnp.where(live_slot, slot_gates, 0.0)
    flat_index = safe_index.reshape(-1)
    picked = second_low[flat_index].reshape(EXPERTS, CAP, D)
    gate_cube = gate_w.reshape(D, EXPERTS, FF)
    up_cube = up_w.reshape(D, EXPERTS, FF)
    down_cube = down_w.reshape(D, EXPERTS, FF)
    gate_pre = low_back(jnp.einsum('ecd,def->ecf', picked, gate_cube, precision=highest))
    up_pre = low_back(jnp.einsum('ecd,def->ecf', picked, up_cube, precision=highest))
    inner_act = low(jax.nn.silu(gate_pre) * up_pre)
    slot_out = low_back(jnp.einsum('ecf,def->ecd', inner_act, down_cube, precision=highest))
    weighted = (slot_out * slot_weight[:, :, None]).reshape(EXPERTS * CAP, D)
    expert_sum = jnp.zeros((seq_length, D), jnp.float32).at[flat_index].add(weighted)
    return hidden + expert_sum

def reference(tokens, segments, slots, gate_values, gains, w_query, w_key, w_value, w_out, w_gate, w_up, w_down, cotangent):
    resid_all = tokens.astype(jnp.float32).reshape(GROUPS, TOK_DEV, D)
    seg_groups = segments.reshape(GROUPS, TOK_DEV)

    def forward(resid_in, gain_rows, query_w, key_w, value_w, out_w, gate_w, up_w, down_w):

        def one_sequence(inputs):
            seq_resid, seq_ids, seq_slots, seq_gates = inputs
            return sequence_layer(seq_resid, seq_ids, seq_slots, seq_gates, gain_rows, query_w, key_w, value_w, out_w, gate_w, up_w, down_w)
        return lax.map(jax.checkpoint(one_sequence), (resid_in, seg_groups, slots, gate_values))
    outputs, pullback = jax.vjp(forward, resid_all, gains.astype(jnp.float32), w_query.astype(jnp.float32), w_key.astype(jnp.float32), w_value.astype(jnp.float32), w_out.astype(jnp.float32), w_gate.astype(jnp.float32), w_up.astype(jnp.float32), w_down.astype(jnp.float32))
    grads = pullback(cotangent.astype(jnp.float32).reshape(GROUPS, TOK_DEV, D))
    return (outputs.reshape(TOKENS, D).astype(jnp.bfloat16), grads[0].reshape(TOKENS, D), grads[1], grads[2], grads[3], grads[4], grads[5], grads[6], grads[7], grads[8])
```

```python
import functools

import jax
import jax.numpy as jnp
from jax import lax
from jax.experimental import pallas as pl
from jax.experimental.pallas import tpu as pltpu
from jax.sharding import PartitionSpec as P

HEAD_DIM = 64
FF = 512
EPS = 1e-06
SUB = 4
TILE = 256
NEG = -1e30
VMEM_BYTES = 56 * 1024 * 1024
BF = jnp.bfloat16
F32 = jnp.float32


def params(*semantics):
    return pltpu.CompilerParams(
        vmem_limit_bytes=VMEM_BYTES, dimension_semantics=semantics or None
    )


def cost(flops, moved, exps=0):
    return pl.CostEstimate(flops=int(flops), bytes_accessed=int(moved), transcendentals=int(exps))


def dot(left, right, left_dim=1, right_dim=0):
    return lax.dot_general(
        left, right, (((left_dim,), (right_dim,)), ((), ())), preferred_element_type=F32
    )


def fill_bias(bias, seg_row, seg_col):
    length = bias.shape[0]

    @pl.when(pl.program_id(0) == 0)
    def _():
        for start in range(0, length, TILE):
            depth = start + TILE
            key_pos = lax.broadcasted_iota(jnp.int32, (depth, TILE), 0)
            query_pos = lax.broadcasted_iota(jnp.int32, (depth, TILE), 1) + start
            allowed = (query_pos >= key_pos) & (
                seg_col[:depth, :] == seg_row[:, start : start + TILE]
            )
            bias[:depth, start : start + TILE] = jnp.where(allowed, 0.0, NEG)


def attend_kernel(group, qkv_ref, seg_row, seg_col, out_ref, log_ref, bias):
    fill_bias(bias, seg_row, seg_col)
    length = bias.shape[0]
    wide = group * HEAD_DIM
    keys = qkv_ref[wide : wide + HEAD_DIM, :].T
    for head in range(group):
        rows = slice(head * HEAD_DIM, (head + 1) * HEAD_DIM)
        for start in range(0, length, TILE):
            depth = start + TILE
            cols = slice(start, depth)
            query = qkv_ref[rows, cols] * jnp.asarray(HEAD_DIM**-0.5, BF)
            scores = dot(keys[:depth], query) + bias[:depth, cols]
            top = jnp.max(scores, axis=0, keepdims=True)
            expo = jnp.exp(scores - top)
            total = jnp.sum(expo, axis=0, keepdims=True)
            mixed = dot(qkv_ref[wide + HEAD_DIM : wide + 2 * HEAD_DIM, :depth], expo.astype(BF))
            out_ref[rows, cols] = (mixed / total).astype(BF)
            log_ref[0, head : head + 1, cols] = top + jnp.log(total)


def attend(qkv, segments, heads_kv, group):
    length = qkv.shape[1]
    wide = (group + 2) * HEAD_DIM
    return pl.pallas_call(
        functools.partial(attend_kernel, group),
        grid=(heads_kv,),
        in_specs=[
            pl.BlockSpec((wide, length), lambda h: (h, 0)),
            pl.BlockSpec((1, length), lambda h: (0, 0)),
            pl.BlockSpec((length, 1), lambda h: (0, 0)),
        ],
        out_specs=[
            pl.BlockSpec((group * HEAD_DIM, length), lambda h: (h, 0)),
            pl.BlockSpec((1, group, length), lambda h: (h, 0, 0)),
        ],
        out_shape=[
            jax.ShapeDtypeStruct((heads_kv * group * HEAD_DIM, length), BF),
            jax.ShapeDtypeStruct((heads_kv, group, length), F32),
        ],
        scratch_shapes=[pltpu.VMEM((length, length), F32)],
        compiler_params=params("arbitrary"),
        cost_estimate=cost(
            heads_kv * group * length * length * HEAD_DIM * 12,
            4 * qkv.size,
            heads_kv * group * length * length,
        ),
        name="attend",
    )(qkv, segments.reshape(1, -1), segments.reshape(-1, 1))


def attend_back_kernel(
    group, qkv_ref, grad_ref, out_ref, log_ref, seg_row, seg_col, back_ref, bias, key_sum, value_sum
):
    fill_bias(bias, seg_row, seg_col)
    length = bias.shape[0]
    wide = group * HEAD_DIM
    scale = HEAD_DIM**-0.5
    keys_t = qkv_ref[wide : wide + HEAD_DIM, :]
    keys = keys_t.T
    values = qkv_ref[wide + HEAD_DIM : wide + 2 * HEAD_DIM, :].T
    key_sum[...] = jnp.zeros_like(key_sum)
    value_sum[...] = jnp.zeros_like(value_sum)
    for head in range(group):
        rows = slice(head * HEAD_DIM, (head + 1) * HEAD_DIM)
        for start in range(0, length, TILE):
            depth = start + TILE
            cols = slice(start, depth)
            query_t = qkv_ref[rows, cols] * jnp.asarray(scale, BF)
            grad_t = grad_ref[rows, cols]
            centre = jnp.sum(
                grad_t.astype(F32) * out_ref[rows, cols].astype(F32), axis=0, keepdims=True
            )
            scores = dot(keys[:depth], query_t) + bias[:depth, cols]
            prob = jnp.exp(scores - log_ref[0, head : head + 1, cols])
            prob_grad = dot(values[:depth], grad_t)
            score_grad = (prob * (prob_grad - centre)).astype(BF)
            back_ref[rows, cols] = (dot(keys_t[:, :depth], score_grad) * scale).astype(BF)
            key_sum[:depth, :] += dot(score_grad, query_t.T)
            value_sum[:depth, :] += dot(prob.astype(BF), grad_t.T)
    back_ref[wide : wide + HEAD_DIM, :] = key_sum[...].T.astype(BF)
    back_ref[wide + HEAD_DIM : wide + 2 * HEAD_DIM, :] = value_sum[...].T.astype(BF)


def attend_back(qkv, grads, attended, logs, segments, heads_kv, group):
    length = qkv.shape[1]
    wide = (group + 2) * HEAD_DIM
    head_block = pl.BlockSpec((group * HEAD_DIM, length), lambda h: (h, 0))
    return pl.pallas_call(
        functools.partial(attend_back_kernel, group),
        grid=(heads_kv,),
        in_specs=[
            pl.BlockSpec((wide, length), lambda h: (h, 0)),
            head_block,
            head_block,
            pl.BlockSpec((1, group, length), lambda h: (h, 0, 0)),
            pl.BlockSpec((1, length), lambda h: (0, 0)),
            pl.BlockSpec((length, 1), lambda h: (0, 0)),
        ],
        out_specs=pl.BlockSpec((wide, length), lambda h: (h, 0)),
        out_shape=jax.ShapeDtypeStruct(qkv.shape, BF),
        scratch_shapes=[
            pltpu.VMEM((length, length), F32),
            pltpu.VMEM((length, HEAD_DIM), F32),
            pltpu.VMEM((length, HEAD_DIM), F32),
        ],
        compiler_params=params("arbitrary"),
        cost_estimate=cost(
            heads_kv * group * length * length * HEAD_DIM * 30,
            8 * qkv.size,
            heads_kv * group * length * length,
        ),
        name="attend_back",
    )(qkv, grads, attended, logs, segments.reshape(1, -1), segments.reshape(-1, 1))


def pick_kernel(index_ref, weight_ref, table_ref, out_ref):
    width = table_ref.shape[0]
    marks = lax.broadcasted_iota(jnp.int32, (index_ref.shape[0], width), 1) == index_ref[...]
    picked = dot(marks.astype(BF), table_ref[...])
    if weight_ref is not None:
        picked = picked * weight_ref[...]
    out_ref[0] = picked.astype(BF)


def pick_plain_kernel(index_ref, table_ref, out_ref):
    pick_kernel(index_ref, None, table_ref, out_ref)


def pick(table, index_col, weight_col, experts):
    cap = index_col.shape[0] // experts
    length, width = table.shape
    column = pl.BlockSpec((cap, 1), lambda e: (e, 0))
    weighted = weight_col is not None
    return pl.pallas_call(
        pick_kernel if weighted else pick_plain_kernel,
        grid=(experts,),
        in_specs=[column] * (2 if weighted else 1)
        + [pl.BlockSpec((length, width), lambda e: (0, 0))],
        out_specs=pl.BlockSpec((1, cap, width), lambda e: (e, 0, 0)),
        out_shape=jax.ShapeDtypeStruct((experts, cap, width), BF),
        compiler_params=params("arbitrary"),
        cost_estimate=cost(
            2 * experts * cap * length * width, 2 * (length + experts * cap) * width
        ),
        name="pick_rows",
    )(*((index_col, weight_col) if weighted else (index_col,)), table)


def put_kernel(experts, index_ref, *refs):
    parts, out_ref = refs[:experts], refs[experts]
    cap = parts[0].shape[1]
    first = pl.program_id(0) * out_ref.shape[0]
    total = None
    for expert in range(experts):
        index = index_ref[:, expert * cap : (expert + 1) * cap]
        marks = lax.broadcasted_iota(jnp.int32, (out_ref.shape[0], cap), 0) + first == index
        part = dot(marks.astype(BF), parts[expert][0])
        total = part if total is None else total + part
    out_ref[...] = total.astype(BF)


def put(parts, index_row, which, length):
    experts = len(parts)
    cap, width = parts[0].shape[1:]
    return pl.pallas_call(
        functools.partial(put_kernel, experts),
        grid=(length // TILE,),
        in_specs=[pl.BlockSpec((1, experts * cap), lambda r: (0, 0))]
        + [pl.BlockSpec((1, cap, width), lambda r: (which, 0, 0))] * experts,
        out_specs=pl.BlockSpec((TILE, width), lambda r: (r, 0)),
        out_shape=jax.ShapeDtypeStruct((length, width), BF),
        compiler_params=params("arbitrary"),
        cost_estimate=cost(
            2 * experts * cap * length * width, 2 * (length + experts * cap) * width
        ),
        name="put_rows",
    )(index_row, *parts)


def expert_kernel(expert, blocks, at_ref, weight_ref, *refs):
    picks, grads, shards = refs[:SUB], refs[SUB : 2 * SUB], refs[2 * SUB : 2 * SUB + blocks]
    refs = refs[2 * SUB + blocks :]
    slot_out, pick_grad, backs = refs[0], refs[1], refs[2 : 2 + blocks]
    picked, slot_grad, gate_w, up_w, down_w, acts, hid_grads, sems = refs[2 + blocks :]
    cap = slot_out.shape[1]
    deep = shards[0].shape[1]
    copies = []
    for k in range(SUB):
        rows = pl.ds(k * cap, cap)
        copies.append(pltpu.make_async_copy(picks[k].at[expert], picked.at[rows], sems.at[2 * k]))
        copies.append(
            pltpu.make_async_copy(grads[k].at[expert], slot_grad.at[rows], sems.at[2 * k + 1])
        )
    for copy in copies:
        copy.start()
    offsets = []
    for r in range(blocks):
        offset = pl.multiple_of(lax.rem(at_ref[0] + r, blocks) * deep, deep)
        offsets.append(offset)
        for held, which in ((gate_w, 0), (up_w, 1), (down_w, 2)):
            held[pl.ds(offset, deep), :] = shards[r][which]
    for copy in copies:
        copy.wait()

    def one(k, carry):
        rows = pl.ds(pl.multiple_of(k * cap, cap), cap)
        weight = weight_ref[rows, :]
        gate_pre = dot(picked[rows, :], gate_w[...])
        up_pre = dot(picked[rows, :], up_w[...])
        sig = 1.0 / (1.0 + jnp.exp(-gate_pre))
        silu = gate_pre * sig
        act = (silu * up_pre).astype(BF)
        acts[rows, :] = act
        slot_out[k] = (dot(act, down_w[...], 1, 1) * weight).astype(BF)
        inner = dot(slot_grad[rows, :], down_w[...])
        gate_grad = (inner * up_pre * sig * (1.0 + gate_pre * (1.0 - sig))).astype(BF)
        up_grad = (inner * silu).astype(BF)
        hid_grads[rows, :FF] = gate_grad
        hid_grads[rows, FF:] = up_grad
        pick_grad[k] = (dot(gate_grad, gate_w[...], 1, 1) + dot(up_grad, up_w[...], 1, 1)).astype(
            BF
        )
        return carry

    lax.fori_loop(0, SUB, one, 0)
    for r in range(blocks):
        cols = pl.ds(offsets[r], deep)
        both = dot(picked[:, cols], hid_grads[...], 0, 0)
        backs[r][0] = both[:, :FF].astype(BF)
        backs[r][1] = both[:, FF:].astype(BF)
        backs[r][2] = dot(slot_grad[:, cols], acts[...], 0, 0).astype(BF)


def run_expert(expert, at, weight_col, picks, grads, shards):
    blocks = len(shards)
    cap, width = picks[0].shape[1:]
    slots = SUB * cap
    whole = pl.BlockSpec(memory_space=pltpu.VMEM)
    return pl.pallas_call(
        functools.partial(expert_kernel, expert, blocks),
        in_specs=[pl.BlockSpec(memory_space=pltpu.SMEM), whole]
        + [pl.BlockSpec(memory_space=pl.ANY)] * (2 * SUB)
        + [whole] * blocks,
        out_specs=[whole] * (2 + blocks),
        out_shape=[jax.ShapeDtypeStruct((SUB, cap, width), BF)] * 2
        + [jax.ShapeDtypeStruct(shards[0].shape, BF)] * blocks,
        scratch_shapes=[
            pltpu.VMEM((slots, width), BF),
            pltpu.VMEM((slots, width), BF),
            pltpu.VMEM((width, FF), BF),
            pltpu.VMEM((width, FF), BF),
            pltpu.VMEM((width, FF), BF),
            pltpu.VMEM((slots, FF), BF),
            pltpu.VMEM((slots, 2 * FF), BF),
            pltpu.SemaphoreType.DMA((2 * SUB,)),
        ],
        compiler_params=params(),
        cost_estimate=cost(18 * slots * width * FF, 8 * slots * width + 12 * width * FF),
        name="expert",
    )(at, weight_col, *picks, *grads, *shards)


def norm_scale(values):
    return lax.rsqrt(jnp.mean(values * values, axis=-1, keepdims=True) + EPS)


def norm_backward(values, rms_scale, gain_row, gradient):
    weighted = gradient * gain_row
    centre = jnp.mean(weighted * values, axis=-1, keepdims=True)
    back_values = rms_scale * weighted - values * rms_scale * rms_scale * rms_scale * centre
    return (back_values, jnp.sum(gradient * values * rms_scale, axis=0))


def layer(
    fsdp,
    tp,
    tokens,
    segments,
    slots,
    gate_values,
    gains,
    w_query,
    w_key,
    w_value,
    w_out,
    w_gate,
    w_up,
    w_down,
    cotangent,
):
    length, width = segments.shape[0], tokens.shape[1]
    half = tokens.shape[0]
    planes = fsdp // SUB
    at_fsdp, at_tp = lax.axis_index("fsdp"), lax.axis_index("tp")
    sub, plane = at_fsdp % SUB, at_fsdp // SUB
    heads_kv = w_key.shape[1] // HEAD_DIM
    group = w_query.shape[1] // w_key.shape[1]
    experts = slots.shape[1] // SUB
    cap = slots.shape[2]

    def swap(values, mask, axis="fsdp"):
        size = fsdp if axis == "fsdp" else tp
        return lax.ppermute(values, axis, [(i, i ^ mask) for i in range(size)])

    def shift(values, planes_on):
        return lax.ppermute(
            values, "fsdp", [(i, (i + planes_on * SUB) % fsdp) for i in range(fsdp)]
        )

    def by_sub(pieces):
        near = [jnp.where((sub & 1) == 1, pieces[k ^ 1], pieces[k]) for k in range(SUB)]
        return [jnp.where((sub & 2) == 2, near[k ^ 2], near[k]) for k in range(SUB)]

    def ordered(mine, other):
        return jnp.where(
            at_tp == 0, jnp.concatenate([mine, other]), jnp.concatenate([other, mine])
        )

    def sequence_gather(mine):
        if tp == 2:
            return ordered(mine, swap(mine, 1, "tp"))
        return lax.all_gather(mine, "tp", axis=0, tiled=True)

    def part_of(values, which):
        return lax.dynamic_slice_in_dim(values, which * half, half, 0)

    def sequence_scatter(values):
        if tp == 2:
            other = swap(part_of(values, 1 - at_tp).astype(BF), 1, "tp")
            return part_of(values, at_tp) + other.astype(F32)
        return lax.psum_scatter(values, "tp", scatter_dimension=0, tiled=True)

    def plane_gather(mine):
        if tp == 2:
            beside, across = swap(mine, 1, "tp"), swap(mine, 2)
            corner = swap(beside, 2)
            first, third = ordered(mine, beside), ordered(across, corner)
        else:
            first = lax.all_gather(mine, "tp", axis=0, tiled=True)
            third = swap(first, 2)
        return [first, swap(first, 1), third, swap(third, 1)]

    def plane_scatter(put_one):
        second, fourth = put_one(1), put_one(3)
        second, fourth = swap(second, 1), swap(fourth, 1)
        third = put_one(2).astype(F32) + fourth.astype(F32)
        if tp == 2:
            corner = swap(part_of(third, 1 - at_tp).astype(BF), 2)
            across = swap(part_of(third, at_tp).astype(BF), 2)
            first = put_one(0).astype(F32) + second.astype(F32)
            beside = part_of(first, 1 - at_tp) + corner.astype(F32)
            beside = swap(beside.astype(BF), 1, "tp")
            return part_of(first, at_tp) + across.astype(F32) + beside.astype(F32)
        first = put_one(0).astype(F32) + second.astype(F32)
        first = first + swap(third.astype(BF), 2).astype(F32)
        return lax.psum_scatter(first, "tp", scatter_dimension=0, tiled=True)

    all_gains = gains
    for axis, size, at in (("tp", tp, at_tp), ("fsdp", fsdp, at_fsdp)):
        mask = 1
        while mask < size:
            other = swap(all_gains, mask, axis)
            all_gains = jnp.where(
                (at & mask) != 0,
                jnp.concatenate([other, all_gains], axis=1),
                jnp.concatenate([all_gains, other], axis=1),
            )
            mask *= 2

    rows = w_query.shape[0]
    packed = jnp.concatenate(
        [
            w_query.reshape(rows, heads_kv, group * HEAD_DIM),
            w_key.reshape(rows, heads_kv, HEAD_DIM),
            w_value.reshape(rows, heads_kv, HEAD_DIM),
        ],
        axis=2,
    ).reshape(rows, -1)
    qkv_cols = packed.shape[1]
    attn_w = lax.all_gather(
        jnp.concatenate([packed, w_out], axis=1), "fsdp", axis=0, tiled=True
    )
    qkv_w, out_w = attn_w[:, :qkv_cols], attn_w[:, qkv_cols:]

    live = slots[0] >= 0
    table = jnp.stack([slots[0].astype(F32), jnp.where(live, gate_values[0], 0.0)])

    def table_for(k):
        return lax.dynamic_slice_in_dim(table, (sub ^ k) * experts, experts, 1)

    tables = [table_for(0)] + [swap(table_for(k), k) for k in range(1, SUB)]
    index = [t[0].astype(jnp.int32) for t in tables]
    index_col = [v.reshape(-1, 1) for v in index]
    index_row = [v.reshape(1, -1) for v in index]
    slot_weight = [t[1] for t in tables]

    def shards_of(expert):
        def piece(k):
            column = ((sub ^ k) * experts + expert) * FF
            return jnp.stack(
                [lax.dynamic_slice_in_dim(w, column, FF, 1) for w in (w_gate, w_up, w_down)]
            )

        pieces = [piece(0)] + [swap(piece(k), k) for k in range(1, SUB)]
        mine = jnp.concatenate(by_sub(pieces), axis=1)
        return [mine] + [shift(mine, -r) for r in range(1, planes)]

    shards = [shards_of(expert) for expert in range(experts)]

    whole_tokens = sequence_gather(tokens).astype(F32)
    first_low = (whole_tokens * norm_scale(whole_tokens) * all_gains[0]).astype(BF)
    qkv = dot(qkv_w, first_low, 0, 1).astype(BF)
    attended, logs = attend(qkv, segments, heads_kv, group)
    resid = tokens.astype(F32)
    hidden = resid + sequence_scatter(dot(attended, out_w, 0, 1))
    scale_two = norm_scale(hidden)
    second_low = (hidden * scale_two * all_gains[1]).astype(BF)

    cots = plane_gather(cotangent)
    slot_grads = [
        pick(cots[k], index_col[k], slot_weight[k].reshape(-1, 1), experts) for k in range(SUB)
    ]
    seconds = plane_gather(second_low)
    picks = [pick(seconds[k], index_col[k], None, experts) for k in range(SUB)]
    at = plane.astype(jnp.int32).reshape(1)
    slot_outs, pick_grads, sums = [], [], []
    for expert in range(experts):
        weight_col = jnp.stack([w[expert] for w in slot_weight]).reshape(-1, 1)
        slot_out, pick_grad, *backs = run_expert(
            expert, at, weight_col, picks, slot_grads, shards[expert]
        )
        slot_outs.append(slot_out)
        pick_grads.append(pick_grad)
        total = backs[0].astype(F32)
        for r in range(1, planes):
            total = total + shift(backs[r], r).astype(F32)
        own_rows = w_gate.shape[0]
        total = total.reshape(3, SUB, own_rows, FF)

        def rows_for(k):
            return lax.dynamic_index_in_dim(total, sub ^ k, 1, keepdims=False)

        pieces = [rows_for(0)] + [
            swap(rows_for(k).astype(BF), k).astype(F32) for k in range(1, SUB)
        ]
        sums.append(by_sub(pieces))
    expert_grads = [
        jnp.concatenate(
            [sums[expert][owner][which] for owner in range(SUB) for expert in range(experts)],
            axis=1,
        )
        for which in range(3)
    ]
    second_grad = plane_scatter(lambda k: put(pick_grads, index_row[k], k, length))
    expert_sum = plane_scatter(lambda k: put(slot_outs, index_row[k], k, length))
    mixed = (hidden + expert_sum).astype(BF)

    back_two, second_gain = norm_backward(hidden, scale_two, all_gains[1], second_grad)
    grad_hidden = cotangent.astype(F32) + back_two
    hidden_low = sequence_gather(grad_hidden.astype(BF))
    grad_out = dot(hidden_low, attended, 0, 1).astype(BF)
    attended_grad = dot(out_w, hidden_low, 0, 1).astype(BF)
    qkv_grad = attend_back(qkv, attended_grad, attended, logs, segments, heads_kv, group)
    grad_qkv = dot(first_low, qkv_grad, 0, 1).astype(BF)
    first_grad = sequence_scatter(dot(qkv_grad, qkv_w, 0, 1))
    back_one, first_gain = norm_backward(resid, norm_scale(resid), all_gains[0], first_grad)
    grad_tokens = grad_hidden + back_one

    grad_gains = jnp.stack([first_gain, second_gain])
    for axis, size, at_axis in (("fsdp", fsdp, at_fsdp), ("tp", tp, at_tp)):
        mask = size // 2
        while mask:
            low, high = jnp.split(grad_gains, 2, axis=1)
            upper = (at_axis & mask) != 0
            kept, sent = jnp.where(upper, high, low), jnp.where(upper, low, high)
            grad_gains = kept + swap(sent, mask, axis)
            mask //= 2

    grad_out = lax.psum_scatter(grad_out, "fsdp", scatter_dimension=0, tiled=True).astype(F32)
    grad_qkv = lax.psum_scatter(grad_qkv, "fsdp", scatter_dimension=0, tiled=True).astype(F32)
    grad_qkv = grad_qkv.reshape(rows, heads_kv, -1)
    cut = group * HEAD_DIM
    return (
        mixed,
        grad_tokens,
        grad_gains,
        grad_qkv[:, :, :cut].reshape(rows, -1),
        grad_qkv[:, :, cut : cut + HEAD_DIM].reshape(rows, -1),
        grad_qkv[:, :, cut + HEAD_DIM :].reshape(rows, -1),
        grad_out,
        *expert_grads,
    )


def solution(mesh):
    both, split = P(("fsdp", "tp"), None), P("fsdp", "tp")
    experts, feature = P("fsdp", "tp", None), P(None, ("fsdp", "tp"))
    return jax.shard_map(
        functools.partial(layer, mesh.shape["fsdp"], mesh.shape["tp"]),
        mesh=mesh,
        in_specs=(both, P("fsdp"), experts, experts, feature) + (split,) * 7 + (both,),
        out_specs=(both, both, feature) + (split,) * 7,
        check_vma=False,
    )
```

```python
import functools

import jax
import jax.numpy as jnp
from jax import lax
from jax.experimental import pallas as pl
from jax.experimental.pallas import tpu as pltpu
from jax.sharding import PartitionSpec as P

HEAD_DIM = 64
FF = 512
EPS = 1e-06
SUB = 4
TILE = 256
NEG = -1e30
CHUNKS = (2, 2)
VMEM_BYTES = 56 * 1024 * 1024
BF = jnp.bfloat16
F32 = jnp.float32


def params(*semantics):
    return pltpu.CompilerParams(
        vmem_limit_bytes=VMEM_BYTES, dimension_semantics=semantics or None
    )


def cost(flops, moved, exps=0):
    return pl.CostEstimate(flops=int(flops), bytes_accessed=int(moved), transcendentals=int(exps))


def dot(left, right, left_dim=1, right_dim=0):
    return lax.dot_general(
        left, right, (((left_dim,), (right_dim,)), ((), ())), preferred_element_type=F32
    )


def tie_kernel(*refs):
    pass


def tie(values, others):
    leaves, tree = jax.tree.flatten(values)
    others = jax.tree.leaves(others)
    anywhere = pl.BlockSpec(memory_space=pl.ANY)
    outs = pl.pallas_call(
        tie_kernel,
        in_specs=[anywhere] * (len(leaves) + len(others)),
        out_specs=[anywhere] * len(leaves),
        out_shape=[jax.ShapeDtypeStruct(leaf.shape, leaf.dtype) for leaf in leaves],
        input_output_aliases={i: i for i in range(len(leaves))},
        compiler_params=params(),
        cost_estimate=cost(0, 0),
        name="tie",
    )(*leaves, *others)
    return jax.tree.unflatten(tree, outs)


def fill_bias(bias, seg_row, seg_col):
    length = bias.shape[0]

    @pl.when(pl.program_id(0) == 0)
    def _():
        for start in range(0, length, TILE):
            depth = start + TILE
            key_pos = lax.broadcasted_iota(jnp.int32, (depth, TILE), 0)
            query_pos = lax.broadcasted_iota(jnp.int32, (depth, TILE), 1) + start
            allowed = (query_pos >= key_pos) & (
                seg_col[:depth, :] == seg_row[:, start : start + TILE]
            )
            bias[:depth, start : start + TILE] = jnp.where(allowed, 0.0, NEG)


def attend_kernel(group, qkv_ref, seg_row, seg_col, out_ref, log_ref, bias):
    fill_bias(bias, seg_row, seg_col)
    length = bias.shape[0]
    wide = group * HEAD_DIM
    keys = qkv_ref[wide : wide + HEAD_DIM, :].T
    for head in range(group):
        rows = slice(head * HEAD_DIM, (head + 1) * HEAD_DIM)
        for start in range(0, length, TILE):
            depth = start + TILE
            cols = slice(start, depth)
            query = qkv_ref[rows, cols] * jnp.asarray(HEAD_DIM**-0.5, BF)
            scores = dot(keys[:depth], query) + bias[:depth, cols]
            top = jnp.max(scores, axis=0, keepdims=True)
            expo = jnp.exp(scores - top)
            total = jnp.sum(expo, axis=0, keepdims=True)
            mixed = dot(qkv_ref[wide + HEAD_DIM : wide + 2 * HEAD_DIM, :depth], expo.astype(BF))
            out_ref[rows, cols] = (mixed / total).astype(BF)
            log_ref[0, head : head + 1, cols] = top + jnp.log(total)


def attend(qkv, segments, heads_kv, group):
    length = qkv.shape[1]
    wide = (group + 2) * HEAD_DIM
    return pl.pallas_call(
        functools.partial(attend_kernel, group),
        grid=(heads_kv,),
        in_specs=[
            pl.BlockSpec((wide, length), lambda h: (h, 0)),
            pl.BlockSpec((1, length), lambda h: (0, 0)),
            pl.BlockSpec((length, 1), lambda h: (0, 0)),
        ],
        out_specs=[
            pl.BlockSpec((group * HEAD_DIM, length), lambda h: (h, 0)),
            pl.BlockSpec((1, group, length), lambda h: (h, 0, 0)),
        ],
        out_shape=[
            jax.ShapeDtypeStruct((heads_kv * group * HEAD_DIM, length), BF),
            jax.ShapeDtypeStruct((heads_kv, group, length), F32),
        ],
        scratch_shapes=[pltpu.VMEM((length, length), F32)],
        compiler_params=params("arbitrary"),
        cost_estimate=cost(
            heads_kv * group * length * length * HEAD_DIM * 12,
            4 * qkv.size,
            heads_kv * group * length * length,
        ),
        name="attend",
    )(qkv, segments.reshape(1, -1), segments.reshape(-1, 1))


def attend_back_kernel(
    group, qkv_ref, grad_ref, out_ref, log_ref, seg_row, seg_col, back_ref, bias, key_sum, value_sum
):
    fill_bias(bias, seg_row, seg_col)
    length = bias.shape[0]
    wide = group * HEAD_DIM
    scale = HEAD_DIM**-0.5
    keys_t = qkv_ref[wide : wide + HEAD_DIM, :]
    keys = keys_t.T
    values = qkv_ref[wide + HEAD_DIM : wide + 2 * HEAD_DIM, :].T
    key_sum[...] = jnp.zeros_like(key_sum)
    value_sum[...] = jnp.zeros_like(value_sum)
    for head in range(group):
        rows = slice(head * HEAD_DIM, (head + 1) * HEAD_DIM)
        for start in range(0, length, TILE):
            depth = start + TILE
            cols = slice(start, depth)
            query_t = qkv_ref[rows, cols] * jnp.asarray(scale, BF)
            grad_t = grad_ref[rows, cols]
            centre = jnp.sum(
                grad_t.astype(F32) * out_ref[rows, cols].astype(F32), axis=0, keepdims=True
            )
            scores = dot(keys[:depth], query_t) + bias[:depth, cols]
            prob = jnp.exp(scores - log_ref[0, head : head + 1, cols])
            prob_grad = dot(values[:depth], grad_t)
            score_grad = (prob * (prob_grad - centre)).astype(BF)
            back_ref[rows, cols] = (dot(keys_t[:, :depth], score_grad) * scale).astype(BF)
            key_sum[:depth, :] += dot(score_grad, query_t.T)
            value_sum[:depth, :] += dot(prob.astype(BF), grad_t.T)
    back_ref[wide : wide + HEAD_DIM, :] = key_sum[...].T.astype(BF)
    back_ref[wide + HEAD_DIM : wide + 2 * HEAD_DIM, :] = value_sum[...].T.astype(BF)


def attend_back(qkv, grads, attended, logs, segments, heads_kv, group):
    length = qkv.shape[1]
    wide = (group + 2) * HEAD_DIM
    head_block = pl.BlockSpec((group * HEAD_DIM, length), lambda h: (h, 0))
    return pl.pallas_call(
        functools.partial(attend_back_kernel, group),
        grid=(heads_kv,),
        in_specs=[
            pl.BlockSpec((wide, length), lambda h: (h, 0)),
            head_block,
            head_block,
            pl.BlockSpec((1, group, length), lambda h: (h, 0, 0)),
            pl.BlockSpec((1, length), lambda h: (0, 0)),
            pl.BlockSpec((length, 1), lambda h: (0, 0)),
        ],
        out_specs=pl.BlockSpec((wide, length), lambda h: (h, 0)),
        out_shape=jax.ShapeDtypeStruct(qkv.shape, BF),
        scratch_shapes=[
            pltpu.VMEM((length, length), F32),
            pltpu.VMEM((length, HEAD_DIM), F32),
            pltpu.VMEM((length, HEAD_DIM), F32),
        ],
        compiler_params=params("arbitrary"),
        cost_estimate=cost(
            heads_kv * group * length * length * HEAD_DIM * 30,
            8 * qkv.size,
            heads_kv * group * length * length,
        ),
        name="attend_back",
    )(qkv, grads, attended, logs, segments.reshape(1, -1), segments.reshape(-1, 1))


def pick_kernel(weighted, parts, index_ref, *refs):
    tables, out_ref = refs[int(weighted) : int(weighted) + parts], refs[-1]
    picked, start = None, 0
    for table in tables:
        count = table.shape[0]
        places = lax.broadcasted_iota(jnp.int32, (index_ref.shape[0], count), 1) + start
        part = dot((places == index_ref[...]).astype(BF), table[...])
        picked = part if picked is None else picked + part
        start += count
    if weighted:
        picked = picked * refs[0][...]
    out_ref[0, 0] = picked.astype(BF)


def pick(tables, index_cols, weight_cols, experts):
    cap = index_cols[0].shape[0] // experts
    width = tables[0][0].shape[1]
    column = pl.BlockSpec((cap, 1), lambda e: (e, 0))
    weighted = weight_cols is not None
    held = None
    for k, parts in enumerate(tables):
        args = [index_cols[k]] + ([weight_cols[k]] if weighted else []) + list(parts)
        specs = [column] * (len(args) - len(parts))
        specs += [pl.BlockSpec(part.shape, lambda e: (0, 0)) for part in parts]
        length = sum(part.shape[0] for part in parts)
        if held is not None:
            args.append(held)
            specs.append(pl.BlockSpec(memory_space=pl.ANY))
        held = pl.pallas_call(
            functools.partial(pick_kernel, weighted, len(parts)),
            grid=(experts,),
            in_specs=specs,
            out_specs=pl.BlockSpec((1, 1, cap, width), lambda e, k=k: (e, k, 0, 0)),
            out_shape=jax.ShapeDtypeStruct((experts, len(tables), cap, width), BF),
            input_output_aliases={} if k == 0 else {len(args) - 1: 0},
            compiler_params=params("arbitrary"),
            cost_estimate=cost(
                2 * experts * cap * length * width, 2 * (length + experts * cap) * width
            ),
            name="pick_rows",
        )(*args)
    return held


def put_kernel(start, added, index_ref, *refs):
    parts, out_ref = refs[: len(refs) - 1 - int(added)], refs[-1]
    cap = parts[0].shape[2]
    first = start + pl.program_id(0) * out_ref.shape[0]
    total, at = (refs[-2][...].astype(F32) if added else None), 0
    for held in parts:
        for expert in range(held.shape[0]):
            index = index_ref[:, at : at + cap]
            marks = lax.broadcasted_iota(jnp.int32, (out_ref.shape[0], cap), 0) + first == index
            part = dot(marks.astype(BF), held[expert, 0])
            total = part if total is None else total + part
            at += cap
    out_ref[...] = total.astype(out_ref.dtype)


def put(parts, index_row, which, start, count, addend=None, kind=BF):
    slots = index_row.shape[1]
    cap, width = parts[0].shape[2:]
    tile = min(TILE, count)
    in_specs = [pl.BlockSpec((1, slots), lambda r: (0, 0))]
    in_specs += [
        pl.BlockSpec((p.shape[0], 1, cap, width), lambda r: (0, which, 0, 0)) for p in parts
    ]
    added = addend is not None
    if added:
        in_specs.append(pl.BlockSpec((tile, width), lambda r: (start // tile + r, 0)))
    return pl.pallas_call(
        functools.partial(put_kernel, start, added),
        grid=(count // tile,),
        in_specs=in_specs,
        out_specs=pl.BlockSpec((tile, width), lambda r: (r, 0)),
        out_shape=jax.ShapeDtypeStruct((count, width), kind),
        compiler_params=params("arbitrary"),
        cost_estimate=cost(2 * slots * count * width, 2 * (count + slots) * width),
        name="put_rows",
    )(index_row, *parts, *([addend] if added else []))


def expert_kernel(
    weight_ref, picked, slot_grad, shards, slot_out, pick_grad, backs, acts, hid_grads
):
    cap, width = picked.shape[2:]
    planes, deep = shards.shape[0], shards.shape[3]

    def weights(which):
        return shards[:, 0, which].reshape(width, FF)

    def one(k, carry):
        rows = pl.ds(pl.multiple_of(k * cap, cap), cap)
        weight = weight_ref[0, rows, :]
        gate_pre = dot(picked[0, k], weights(0))
        up_pre = dot(picked[0, k], weights(1))
        sig = 1.0 / (1.0 + jnp.exp(-gate_pre))
        silu = gate_pre * sig
        act = (silu * up_pre).astype(BF)
        acts[rows, :] = act
        slot_out[0, k] = (dot(act, weights(2), 1, 1) * weight).astype(BF)
        inner = dot(slot_grad[0, k], weights(2))
        gate_grad = (inner * up_pre * sig * (1.0 + gate_pre * (1.0 - sig))).astype(BF)
        up_grad = (inner * silu).astype(BF)
        hid_grads[rows, :FF] = gate_grad
        hid_grads[rows, FF:] = up_grad
        pick_grad[0, k] = (
            dot(gate_grad, weights(0), 1, 1) + dot(up_grad, weights(1), 1, 1)
        ).astype(BF)
        return carry

    lax.fori_loop(0, SUB, one, 0)
    for plane in range(planes):
        cols = slice(plane * deep, (plane + 1) * deep)
        mine = picked[0, :, :, cols].reshape(SUB * cap, deep)
        both = dot(mine, hid_grads[...], 0, 0)
        backs[plane, 0, 0] = both[:, :FF].astype(BF)
        backs[plane, 0, 1] = both[:, FF:].astype(BF)
        mine = slot_grad[0, :, :, cols].reshape(SUB * cap, deep)
        backs[plane, 0, 2] = dot(mine, acts[...], 0, 0).astype(BF)


def run_experts(first, weight_col, picked, slot_grads, shards):
    planes, count, _, deep, _ = shards.shape
    cap, width = picked.shape[2:]
    slots = SUB * cap
    rows = pl.BlockSpec((1, SUB, cap, width), lambda e: (first + e, 0, 0, 0))
    out_rows = pl.BlockSpec((1, SUB, cap, width), lambda e: (e, 0, 0, 0))
    block = pl.BlockSpec((planes, 1, 3, deep, FF), lambda e: (0, e, 0, 0, 0))
    return pl.pallas_call(
        expert_kernel,
        grid=(count,),
        in_specs=[pl.BlockSpec((1, slots, 1), lambda e: (first + e, 0, 0)), rows, rows, block],
        out_specs=[out_rows, out_rows, block],
        out_shape=[jax.ShapeDtypeStruct((count, SUB, cap, width), BF)] * 2
        + [jax.ShapeDtypeStruct(shards.shape, BF)],
        scratch_shapes=[pltpu.VMEM((slots, FF), BF), pltpu.VMEM((slots, 2 * FF), BF)],
        compiler_params=params("arbitrary"),
        cost_estimate=cost(
            18 * count * slots * width * FF, count * (8 * slots * width + 12 * width * FF)
        ),
        name="experts",
    )(weight_col, picked, slot_grads, shards)


def place_kernel(first, experts, at_ref, *refs):
    pieces, outs, held, sems = refs[:SUB], refs[-5:-2], refs[-2], refs[-1]
    count = pieces[0].shape[0]
    copies = []
    for k in range(SUB):
        owner = lax.bitwise_xor(at_ref[0], k)
        for e in range(count):
            column = pl.multiple_of((owner * experts + (first + e)) * FF, FF)
            for which, out in enumerate(outs):
                at = len(copies)
                held[at] = pieces[k][e, which].astype(F32)
                copy = pltpu.make_async_copy(
                    held.at[at], out.at[:, pl.ds(column, FF)], sems.at[at]
                )
                copy.start()
                copies.append(copy)
    for copy in copies:
        copy.wait()


def place(sub, pieces, first, experts, held):
    count, _, rows, _ = pieces[0].shape
    anywhere = pl.BlockSpec(memory_space=pl.ANY)
    in_specs = [pl.BlockSpec(memory_space=pltpu.SMEM)]
    in_specs += [pl.BlockSpec(memory_space=pltpu.VMEM)] * SUB
    held = list(held or ())
    return pl.pallas_call(
        functools.partial(place_kernel, first, experts),
        in_specs=in_specs + [anywhere] * len(held),
        out_specs=[anywhere] * 3,
        out_shape=[jax.ShapeDtypeStruct((rows, SUB * experts * FF), F32)] * 3,
        scratch_shapes=[
            pltpu.VMEM((3 * SUB * count, rows, FF), F32),
            pltpu.SemaphoreType.DMA((3 * SUB * count,)),
        ],
        input_output_aliases={1 + SUB + i: i for i in range(len(held))},
        compiler_params=params(),
        cost_estimate=cost(0, 18 * SUB * count * rows * FF),
        name="place_rows",
    )(sub.astype(jnp.int32).reshape(1), *pieces, *held)


def norm_scale(values):
    return lax.rsqrt(jnp.mean(values * values, axis=-1, keepdims=True) + EPS)


def norm_backward(values, rms_scale, gain_row, gradient):
    weighted = gradient * gain_row
    centre = jnp.mean(weighted * values, axis=-1, keepdims=True)
    back_values = rms_scale * weighted - values * rms_scale * rms_scale * rms_scale * centre
    return (back_values, jnp.sum(gradient * values * rms_scale, axis=0))


def layer(
    fsdp,
    tp,
    tokens,
    segments,
    slots,
    gate_values,
    gains,
    w_query,
    w_key,
    w_value,
    w_out,
    w_gate,
    w_up,
    w_down,
    cotangent,
):
    length, width = segments.shape[0], tokens.shape[1]
    half = tokens.shape[0]
    planes = fsdp // SUB
    at_fsdp, at_tp = lax.axis_index("fsdp"), lax.axis_index("tp")
    sub, plane = at_fsdp % SUB, at_fsdp // SUB
    heads_kv = w_key.shape[1] // HEAD_DIM
    group = w_query.shape[1] // w_key.shape[1]
    experts = slots.shape[1] // SUB
    cap = slots.shape[2]

    def swap(values, mask, axis="fsdp"):
        size = fsdp if axis == "fsdp" else tp
        return lax.ppermute(values, axis, [(i, i ^ mask) for i in range(size)])

    def shift(values, planes_on):
        return lax.ppermute(
            values, "fsdp", [(i, (i + planes_on * SUB) % fsdp) for i in range(fsdp)]
        )

    def by_sub(pieces):
        near = [jnp.where((sub & 1) == 1, pieces[k ^ 1], pieces[k]) for k in range(SUB)]
        return [jnp.where((sub & 2) == 2, near[k ^ 2], near[k]) for k in range(SUB)]

    def ordered(mine, other):
        return jnp.where(
            at_tp == 0, jnp.concatenate([mine, other]), jnp.concatenate([other, mine])
        )

    def sequence_gather(mine):
        if tp == 2:
            return ordered(mine, swap(mine, 1, "tp"))
        return lax.all_gather(mine, "tp", axis=0, tiled=True)

    def part_of(values, which):
        return lax.dynamic_slice_in_dim(values, which * half, half, 0)

    def sequence_scatter(values):
        if tp == 2:
            other = swap(part_of(values, 1 - at_tp).astype(BF), 1, "tp")
            return part_of(values, at_tp) + other.astype(F32)
        return lax.psum_scatter(values, "tp", scatter_dimension=0, tiled=True)

    turn = half * at_tp if tp == 2 else 0

    def plane_start(mine):
        if tp == 2:
            return swap(mine, 1, "tp"), swap(mine, 2)
        return (lax.all_gather(mine, "tp", axis=0, tiled=True),)

    def plane_finish(mine, begun):
        if tp == 2:
            beside, across = begun
            first, third = (mine, beside), (across, swap(beside, 2))
        else:
            first = begun
            third = (swap(first[0], 2),)
        return [first, [swap(p, 1) for p in first], third, [swap(p, 1) for p in third]]

    def plane_scatter(put_one):
        fourth, second = swap(put_one(3, 0, length), 1), swap(put_one(1, 0, length), 1)
        if tp == 2:
            corner = put_one(2, half, half, fourth)
            across = put_one(2, 0, half, fourth)
            other = put_one(0, half, half, second, F32)
            mine = put_one(0, 0, half, second, F32)

            def finish(got):
                corner, across = got
                beside = swap((other + corner.astype(F32)).astype(BF), 1, "tp")
                return mine + across.astype(F32) + beside.astype(F32)

            return (swap(corner, 2), swap(across, 2)), (corner, across), finish
        third = put_one(2, 0, length, fourth)
        first = put_one(0, 0, length, second, F32)

        def finish(got):
            total = first + got.astype(F32)
            return lax.psum_scatter(total, "tp", scatter_dimension=0, tiled=True)

        return swap(third, 2), third, finish

    def weight_scatter(values):
        values = values.reshape(planes, 2, 2, -1, values.shape[1])
        core, line = sub & 1, sub >> 1
        sent = lax.dynamic_index_in_dim(values, 1 - core, 2, keepdims=False)
        kept = lax.dynamic_index_in_dim(values, core, 2, keepdims=False)
        values = kept.astype(F32) + swap(sent.astype(BF), 1).astype(F32)
        sent = lax.dynamic_index_in_dim(values, 1 - line, 1, keepdims=False)
        kept = lax.dynamic_index_in_dim(values, line, 1, keepdims=False)
        values = kept + swap(sent.astype(BF), 2).astype(F32)

        total = lax.dynamic_index_in_dim(values, plane, 0, keepdims=False)
        got = [
            shift(
                lax.dynamic_index_in_dim(
                    values, (plane + r) % planes, 0, keepdims=False
                ).astype(BF),
                r,
            )
            for r in range(1, planes)
        ]
        return values, got, lambda got: sum([total] + [part.astype(F32) for part in got])

    def gain_scatter(values):
        values = values.reshape(2, planes, SUB, tp, -1)

        def block(which, axis):
            return lax.dynamic_index_in_dim(values, which, axis, keepdims=False)

        if tp == 2:
            values = block(at_tp, 3) + swap(block(1 - at_tp, 3), 1, "tp")
        else:
            values = lax.psum_scatter(values, "tp", scatter_dimension=3)
        values = sum([block(sub, 2)] + [swap(block(sub ^ k, 2), k) for k in range(1, SUB)])
        return values, lambda values: sum(
            [lax.dynamic_index_in_dim(values, plane, 1, keepdims=False)]
            + [
                shift(
                    lax.dynamic_index_in_dim(values, (plane + r) % planes, 1, keepdims=False), r
                )
                for r in range(1, planes)
            ]
        )

    if tp == 2:
        near_gains = swap(gains, 1, "tp")
        near_gains = jnp.where(
            at_tp == 0,
            jnp.concatenate([gains, near_gains], axis=1),
            jnp.concatenate([near_gains, gains], axis=1),
        )
    else:
        near_gains = lax.all_gather(gains, "tp", axis=1, tiled=True)
    whole_tokens = sequence_gather(tokens)
    plane_gains = jnp.concatenate(
        by_sub([near_gains] + [swap(near_gains, k) for k in range(1, SUB)]), axis=1
    )
    all_gains = jnp.stack([plane_gains] + [shift(plane_gains, -r) for r in range(1, planes)])
    all_gains = jnp.concatenate([all_gains, all_gains])
    all_gains = lax.dynamic_slice_in_dim(all_gains, planes - plane, planes, 0)
    all_gains = all_gains.transpose(1, 0, 2).reshape(2, -1)

    rows = w_query.shape[0]
    packed = jnp.concatenate(
        [
            w_query.reshape(rows, heads_kv, group * HEAD_DIM),
            w_key.reshape(rows, heads_kv, HEAD_DIM),
            w_value.reshape(rows, heads_kv, HEAD_DIM),
        ],
        axis=2,
    ).reshape(rows, -1)
    qkv_cols = packed.shape[1]
    attn_w = lax.all_gather(
        jnp.concatenate([packed, w_out], axis=1), "fsdp", axis=0, tiled=True
    )
    qkv_w, out_w = attn_w[:, :qkv_cols], attn_w[:, qkv_cols:]

    live = slots[0] >= 0
    table = jnp.stack([slots[0].astype(F32), jnp.where(live, gate_values[0], 0.0)])

    def table_for(k):
        return lax.dynamic_slice_in_dim(table, (sub ^ k) * experts, experts, 1)

    tables = [table_for(0)] + [swap(table_for(k), k) for k in range(1, SUB)]
    index = [t[0].astype(jnp.int32) for t in tables]
    index = [jnp.where(v < 0, -1, (v + (length - turn)) % length) for v in index]
    index_col = [v.reshape(-1, 1) for v in index]
    index_row = [v.reshape(1, -1) for v in index]
    slot_weight = [t[1] for t in tables]

    across = [[j + SUB * p for p in range(planes)] for j in range(SUB)]
    chunks, taken = [], 0
    for count in CHUNKS:
        count = min(count, experts - taken)
        if count:
            chunks.append((taken, count))
            taken += count

    def pieces_of(first, count, others):
        def piece(k):
            column = ((sub ^ k) * experts + first) * FF
            cut = [
                lax.dynamic_slice_in_dim(w, column, count * FF, 1).reshape(-1, count, FF)
                for w in (w_gate, w_up, w_down)
            ]
            return jnp.stack(cut).transpose(2, 0, 1, 3)

        sends = tie([piece(k) for k in range(1, SUB)], others)
        return [piece(0)] + [swap(sent, k + 1) for k, sent in enumerate(sends)]

    def shards_of(pieces, others=None):
        if others is not None:
            pieces = [pieces[0]] + tie(pieces[1:], others)
        mine = jnp.concatenate(by_sub(pieces), axis=2)
        return lax.all_gather(mine, "fsdp", axis_index_groups=across), mine

    held, mine_first = shards_of(
        pieces_of(*chunks[0], (plane_gains, tables)), (all_gains, whole_tokens)
    )
    shards = [held]

    whole_resid = whole_tokens.astype(F32)
    first_low = (whole_resid * norm_scale(whole_resid) * all_gains[0]).astype(BF)
    begun = plane_start(tie(cotangent, mine_first))
    qkv = dot(qkv_w, first_low, 0, 1).astype(BF)
    later = [pieces_of(*chunk, qkv) for chunk in chunks[1:]]
    attended, logs = attend(qkv, segments, heads_kv, group)
    begun, later = tie((begun, later), attended)
    shards += [shards_of(pieces)[0] for pieces in later]
    cots = plane_finish(cotangent, begun)
    resid = tokens.astype(F32)
    hidden = resid + sequence_scatter(dot(attended, out_w, 0, 1))
    scale_two = norm_scale(hidden)
    second_low = (hidden * scale_two * all_gains[1]).astype(BF)

    slot_grads = pick(
        cots, index_col, [w.reshape(-1, 1) for w in slot_weight], experts
    )
    picked = pick(
        plane_finish(second_low, plane_start(second_low)), index_col, None, experts
    )
    weight_col = jnp.stack(slot_weight, axis=1).reshape(experts, -1, 1)
    slot_outs, pick_grads, sums = [], [], []
    for (first, count), held in zip(chunks, shards):
        slot_out, pick_grad, backs = run_experts(first, weight_col, picked, slot_grads, held)
        slot_outs.append(slot_out)
        pick_grads.append(pick_grad)
        sums.append(
            lax.psum_scatter(backs, "fsdp", scatter_dimension=0, axis_index_groups=across)
        )
    got, sent, finish = plane_scatter(lambda k, *more: put(pick_grads, index_row[k], k, *more))
    second_grad = finish(got)
    index_row = tie(index_row, sent)
    got_out, _, finish_out_sum = plane_scatter(
        lambda k, *more: put(slot_outs, index_row[k], k, *more)
    )

    back_two, second_gain = norm_backward(hidden, scale_two, all_gains[1], second_grad)
    grad_hidden = cotangent.astype(F32) + back_two
    own_low = grad_hidden.astype(BF)

    def rows_out(part):
        part = part.reshape(-1, 3, SUB, rows, FF)
        return [
            lax.dynamic_index_in_dim(part, sub ^ k, 2, keepdims=False) for k in range(SUB)
        ]

    early = []
    for part in sums[:-1]:
        own, *sends = rows_out(part)
        early.append((own, tie(sends, own_low)))
    if tp == 2:
        other_low = tie(swap(own_low, 1, "tp"), early)
        hidden_low = ordered(own_low, other_low)
    else:
        hidden_low = lax.all_gather(own_low, "tp", axis=0, tiled=True)
    early = [[own] + [swap(sent, k + 1) for k, sent in enumerate(sends)] for own, sends in early]
    _, got_grad_out, finish_out = weight_scatter(dot(hidden_low, attended, 0, 1))
    attended_grad = dot(out_w, hidden_low, 0, 1).astype(BF)
    qkv_grad = attend_back(qkv, attended_grad, attended, logs, segments, heads_kv, group)
    grad_qkv = dot(first_low, qkv_grad, 0, 1)
    first_part = dot(qkv_grad, qkv_w, 0, 1)
    if tp == 2:
        got = swap(part_of(first_part, 1 - at_tp).astype(BF), 1, "tp")
        got, early, got_out = tie((got, early, got_out), ())
        first_grad = part_of(first_part, at_tp) + got.astype(F32)
    else:
        first_grad = sequence_scatter(first_part)
    mixed = (hidden + finish_out_sum(got_out)).astype(BF)
    expert_grads = None
    for number, pieces in enumerate(early):
        expert_grads = place(sub, pieces, chunks[number][0], experts, expert_grads)
    back_one, first_gain = norm_backward(resid, norm_scale(resid), all_gains[0], first_grad)
    grad_tokens = grad_hidden + back_one
    grad_gains, finish_gains = gain_scatter(jnp.stack([first_gain, second_gain]))
    grad_qkv, got_qkv, finish_qkv = weight_scatter(grad_qkv)
    grad_out = finish_out(tie(got_grad_out, grad_qkv))

    own, *sends = rows_out(tie(sums[-1], (grad_qkv, grad_gains)))
    late = [own] + [swap(sent, k + 1) for k, sent in enumerate(sends)]
    expert_grads = place(sub, late, chunks[-1][0], experts, expert_grads)
    grad_gains = finish_gains(grad_gains)
    grad_qkv = finish_qkv(got_qkv).reshape(rows, heads_kv, -1)
    cut = group * HEAD_DIM
    return (
        mixed,
        grad_tokens,
        grad_gains,
        grad_qkv[:, :, :cut].reshape(rows, -1),
        grad_qkv[:, :, cut : cut + HEAD_DIM].reshape(rows, -1),
        grad_qkv[:, :, cut + HEAD_DIM :].reshape(rows, -1),
        grad_out,
        *expert_grads,
    )


def solution(mesh):
    both, split = P(("fsdp", "tp"), None), P("fsdp", "tp")
    experts, feature = P("fsdp", "tp", None), P(None, ("fsdp", "tp"))
    return jax.shard_map(
        functools.partial(layer, mesh.shape["fsdp"], mesh.shape["tp"]),
        mesh=mesh,
        in_specs=(both, P("fsdp"), experts, experts, feature) + (split,) * 7 + (both,),
        out_specs=(both, both, feature) + (split,) * 7,
        check_vma=False,
    )
```

```python
import functools

import jax
import jax.numpy as jnp
from jax import lax
from jax.experimental import pallas as pl
from jax.experimental.pallas import tpu as pltpu
from jax.sharding import PartitionSpec as P

HEAD_DIM = 64
FF = 512
EPS = 1e-06
SUB = 4
TILE = 256
NEG = -1e30
LANES = 128
CHUNKS = (3, 1)
VMEM_BYTES = 56 * 1024 * 1024
BF = jnp.bfloat16
F32 = jnp.float32


def params(*semantics):
    return pltpu.CompilerParams(
        vmem_limit_bytes=VMEM_BYTES, dimension_semantics=semantics or None
    )


def cost(flops, moved, exps=0):
    return pl.CostEstimate(flops=int(flops), bytes_accessed=int(moved), transcendentals=int(exps))


def dot(left, right, left_dim=1, right_dim=0):
    return lax.dot_general(
        left, right, (((left_dim,), (right_dim,)), ((), ())), preferred_element_type=F32
    )


def tie_kernel(*refs):
    pass


def tie(values, others):
    leaves, tree = jax.tree.flatten(values)
    others = jax.tree.leaves(others)
    anywhere = pl.BlockSpec(memory_space=pl.ANY)
    outs = pl.pallas_call(
        tie_kernel,
        in_specs=[anywhere] * (len(leaves) + len(others)),
        out_specs=[anywhere] * len(leaves),
        out_shape=[jax.ShapeDtypeStruct(leaf.shape, leaf.dtype) for leaf in leaves],
        input_output_aliases={i: i for i in range(len(leaves))},
        compiler_params=params(),
        cost_estimate=cost(0, 0),
        name="tie",
    )(*leaves, *others)
    return jax.tree.unflatten(tree, outs)


def move_kernel(plan, sources, at_ref, *refs):
    outs, sems = refs[sources:-1], refs[-1]
    copies = [
        pltpu.make_async_copy(refs[i].at[taken], out.at[put_at], sems.at[number])
        for number, (i, taken, out, put_at) in enumerate(plan(at_ref, outs))
    ]
    for copy in copies:
        copy.start()
    for copy in copies:
        copy.wait()


def move(at, sources, shapes, steps, plan, others=()):
    anywhere = pl.BlockSpec(memory_space=pl.ANY)
    operands = [*sources, *jax.tree.leaves(others)]
    return pl.pallas_call(
        functools.partial(move_kernel, plan, len(operands)),
        in_specs=[pl.BlockSpec(memory_space=pltpu.SMEM)] + [anywhere] * len(operands),
        out_specs=[pl.BlockSpec(memory_space=pltpu.VMEM)] * len(shapes),
        out_shape=[jax.ShapeDtypeStruct(shape, BF) for shape in shapes],
        scratch_shapes=[pltpu.SemaphoreType.DMA((steps,))],
        compiler_params=params(),
        cost_estimate=cost(0, 4 * sum(source.size for source in sources)),
        name="move",
    )(at, *operands)


def fill_bias(bias, seg_row, seg_col):
    length = bias.shape[0]

    @pl.when(pl.program_id(0) == 0)
    def _():
        for start in range(0, length, TILE):
            depth = start + TILE
            key_pos = lax.broadcasted_iota(jnp.int32, (depth, TILE), 0)
            query_pos = lax.broadcasted_iota(jnp.int32, (depth, TILE), 1) + start
            allowed = (query_pos >= key_pos) & (
                seg_col[:depth, :] == seg_row[:, start : start + TILE]
            )
            bias[:depth, start : start + TILE] = jnp.where(allowed, 0.0, NEG)


def attend_kernel(group, qkv_ref, seg_row, seg_col, out_ref, log_ref, bias):
    fill_bias(bias, seg_row, seg_col)
    length = bias.shape[0]
    wide = group * HEAD_DIM
    keys = qkv_ref[wide : wide + HEAD_DIM, :].T
    for head in range(group):
        rows = slice(head * HEAD_DIM, (head + 1) * HEAD_DIM)
        for start in range(0, length, TILE):
            depth = start + TILE
            cols = slice(start, depth)
            query = qkv_ref[rows, cols] * jnp.asarray(HEAD_DIM**-0.5, BF)
            scores = dot(keys[:depth], query) + bias[:depth, cols]
            top = jnp.max(scores, axis=0, keepdims=True)
            expo = jnp.exp(scores - top)
            total = jnp.sum(expo, axis=0, keepdims=True)
            mixed = dot(qkv_ref[wide + HEAD_DIM : wide + 2 * HEAD_DIM, :depth], expo.astype(BF))
            out_ref[rows, cols] = (mixed / total).astype(BF)
            log_ref[0, head : head + 1, cols] = top + jnp.log(total)


def attend(qkv, segments, heads_kv, group):
    length = qkv.shape[1]
    wide = (group + 2) * HEAD_DIM
    return pl.pallas_call(
        functools.partial(attend_kernel, group),
        grid=(heads_kv,),
        in_specs=[
            pl.BlockSpec((wide, length), lambda h: (h, 0)),
            pl.BlockSpec((1, length), lambda h: (0, 0)),
            pl.BlockSpec((length, 1), lambda h: (0, 0)),
        ],
        out_specs=[
            pl.BlockSpec((group * HEAD_DIM, length), lambda h: (h, 0)),
            pl.BlockSpec((1, group, length), lambda h: (h, 0, 0)),
        ],
        out_shape=[
            jax.ShapeDtypeStruct((heads_kv * group * HEAD_DIM, length), BF),
            jax.ShapeDtypeStruct((heads_kv, group, length), F32),
        ],
        scratch_shapes=[pltpu.VMEM((length, length), F32)],
        compiler_params=params("arbitrary"),
        cost_estimate=cost(
            heads_kv * group * length * length * HEAD_DIM * 12,
            4 * qkv.size,
            heads_kv * group * length * length,
        ),
        name="attend",
    )(qkv, segments.reshape(1, -1), segments.reshape(-1, 1))


def attend_back_kernel(
    group, qkv_ref, grad_ref, out_ref, log_ref, seg_row, seg_col, back_ref, bias, key_sum, value_sum
):
    fill_bias(bias, seg_row, seg_col)
    length = bias.shape[0]
    wide = group * HEAD_DIM
    scale = HEAD_DIM**-0.5
    keys_t = qkv_ref[wide : wide + HEAD_DIM, :]
    keys = keys_t.T
    values = qkv_ref[wide + HEAD_DIM : wide + 2 * HEAD_DIM, :].T
    key_sum[...] = jnp.zeros_like(key_sum)
    value_sum[...] = jnp.zeros_like(value_sum)
    for head in range(group):
        rows = slice(head * HEAD_DIM, (head + 1) * HEAD_DIM)
        for start in range(0, length, TILE):
            depth = start + TILE
            cols = slice(start, depth)
            query_t = qkv_ref[rows, cols] * jnp.asarray(scale, BF)
            grad_t = grad_ref[rows, cols]
            centre = jnp.sum(
                grad_t.astype(F32) * out_ref[rows, cols].astype(F32), axis=0, keepdims=True
            )
            scores = dot(keys[:depth], query_t) + bias[:depth, cols]
            prob = jnp.exp(scores - log_ref[0, head : head + 1, cols])
            prob_grad = dot(values[:depth], grad_t)
            score_grad = (prob * (prob_grad - centre)).astype(BF)
            back_ref[rows, cols] = (dot(keys_t[:, :depth], score_grad) * scale).astype(BF)
            key_sum[:depth, :] += dot(score_grad, query_t.T)
            value_sum[:depth, :] += dot(prob.astype(BF), grad_t.T)
    back_ref[wide : wide + HEAD_DIM, :] = key_sum[...].T.astype(BF)
    back_ref[wide + HEAD_DIM : wide + 2 * HEAD_DIM, :] = value_sum[...].T.astype(BF)


def attend_back(qkv, grads, attended, logs, segments, heads_kv, group):
    length = qkv.shape[1]
    wide = (group + 2) * HEAD_DIM
    head_block = pl.BlockSpec((group * HEAD_DIM, length), lambda h: (h, 0))
    return pl.pallas_call(
        functools.partial(attend_back_kernel, group),
        grid=(heads_kv,),
        in_specs=[
            pl.BlockSpec((wide, length), lambda h: (h, 0)),
            head_block,
            head_block,
            pl.BlockSpec((1, group, length), lambda h: (h, 0, 0)),
            pl.BlockSpec((1, length), lambda h: (0, 0)),
            pl.BlockSpec((length, 1), lambda h: (0, 0)),
        ],
        out_specs=pl.BlockSpec((wide, length), lambda h: (h, 0)),
        out_shape=jax.ShapeDtypeStruct(qkv.shape, BF),
        scratch_shapes=[
            pltpu.VMEM((length, length), F32),
            pltpu.VMEM((length, HEAD_DIM), F32),
            pltpu.VMEM((length, HEAD_DIM), F32),
        ],
        compiler_params=params("arbitrary"),
        cost_estimate=cost(
            heads_kv * group * length * length * HEAD_DIM * 30,
            8 * qkv.size,
            heads_kv * group * length * length,
        ),
        name="attend_back",
    )(qkv, grads, attended, logs, segments.reshape(1, -1), segments.reshape(-1, 1))


def pick_kernel(weighted, parts, slot_ref, *refs):
    tables, out_ref = refs[:parts], refs[-1]
    cap = out_ref.shape[2]
    expert = pl.program_id(0)

    def column(which):
        row = slot_ref[which, pl.ds(expert, 1), :]
        return jnp.broadcast_to(row, (LANES, cap)).T

    index = column(0)
    lane = lax.broadcasted_iota(jnp.int32, (cap, LANES), 1).astype(F32)
    picked, start = None, 0
    for table in tables:
        marks = [
            (lane + float(start + at) == index).astype(BF)
            for at in range(0, table.shape[0], LANES)
        ]
        part = dot(jnp.concatenate(marks, axis=1), table[...])
        picked = part if picked is None else picked + part
        start += table.shape[0]
    if weighted:
        picked = picked * column(1)[:, :1]
    out_ref[0, 0] = picked.astype(BF)


def pick(tables, slots, weighted):
    _, experts, cap = slots[0].shape
    width = tables[0][0].shape[1]
    held = None
    for k, parts in enumerate(tables):
        args = [slots[k], *parts]
        specs = [pl.BlockSpec(slots[k].shape, lambda e: (0, 0, 0))]
        specs += [pl.BlockSpec(part.shape, lambda e: (0, 0)) for part in parts]
        length = sum(part.shape[0] for part in parts)
        if held is not None:
            args.append(held)
            specs.append(pl.BlockSpec(memory_space=pl.ANY))
        held = pl.pallas_call(
            functools.partial(pick_kernel, weighted, len(parts)),
            grid=(experts,),
            in_specs=specs,
            out_specs=pl.BlockSpec((1, 1, cap, width), lambda e, k=k: (e, k, 0, 0)),
            out_shape=jax.ShapeDtypeStruct((experts, len(tables), cap, width), BF),
            input_output_aliases={} if k == 0 else {len(args) - 1: 0},
            compiler_params=params("arbitrary"),
            cost_estimate=cost(
                2 * experts * cap * length * width, 2 * (length + experts * cap) * width
            ),
            name="pick_rows",
        )(*args)
    return held


def put_kernel(start, weighted, added, slot_ref, *refs):
    parts, out_ref = refs[: len(refs) - 1 - int(added)], refs[-1]
    cap = parts[0].shape[2]
    first = start + pl.program_id(0) * out_ref.shape[0]
    place = (lax.broadcasted_iota(jnp.int32, (out_ref.shape[0], cap), 0) + first).astype(F32)
    total, at = None, 0
    for held in parts:
        for expert in range(held.shape[0]):
            match = place == slot_ref[0, at : at + 1, :]
            if weighted:
                marks = jnp.where(match, slot_ref[1, at : at + 1, :], 0.0).astype(BF)
            else:
                marks = match.astype(BF)
            part = dot(marks, held[expert, 0])
            total = part if total is None else total + part
            at += 1
    if added:
        total = total + refs[-2][...].astype(F32)
    out_ref[...] = total.astype(out_ref.dtype)


def put(parts, slots, weighted, which, start, count, addends=(), kind=BF):
    cap, width = parts[0].shape[2:]
    tile = min(TILE, count)
    in_specs = [pl.BlockSpec(slots.shape, lambda r: (0, 0, 0))]
    in_specs += [
        pl.BlockSpec((p.shape[0], 1, cap, width), lambda r: (0, which, 0, 0)) for p in parts
    ]
    in_specs += [pl.BlockSpec((tile, width), lambda r: (start // tile + r, 0))] * len(addends)
    moved = slots.shape[1] * cap
    return pl.pallas_call(
        functools.partial(put_kernel, start, weighted, bool(addends)),
        grid=(count // tile,),
        in_specs=in_specs,
        out_specs=pl.BlockSpec((tile, width), lambda r: (r, 0)),
        out_shape=jax.ShapeDtypeStruct((count, width), kind),
        compiler_params=params("arbitrary"),
        cost_estimate=cost(2 * moved * count * width, 2 * (count + moved) * width),
        name="put_rows",
    )(slots, *parts, *addends)


def expert_kernel(
    picked, slot_grad, shards, slot_out, pick_grad, backs, acts, hid_grads
):
    cap, width = picked.shape[2:]
    planes, deep = shards.shape[0], shards.shape[3]

    def weights(which):
        return shards[:, 0, which].reshape(width, FF)

    def one(k, carry):
        rows = pl.ds(pl.multiple_of(k * cap, cap), cap)
        gate_pre = dot(picked[0, k], weights(0))
        up_pre = dot(picked[0, k], weights(1))
        sig = 1.0 / (1.0 + jnp.exp(-gate_pre))
        silu = gate_pre * sig
        act = (silu * up_pre).astype(BF)
        acts[rows, :] = act
        slot_out[0, k] = dot(act, weights(2), 1, 1).astype(BF)
        inner = dot(slot_grad[0, k], weights(2))
        gate_grad = (inner * up_pre * sig * (1.0 + gate_pre * (1.0 - sig))).astype(BF)
        up_grad = (inner * silu).astype(BF)
        hid_grads[rows, :FF] = gate_grad
        hid_grads[rows, FF:] = up_grad
        pick_grad[0, k] = (
            dot(gate_grad, weights(0), 1, 1) + dot(up_grad, weights(1), 1, 1)
        ).astype(BF)
        return carry

    lax.fori_loop(0, SUB, one, 0)
    for plane in range(planes):
        cols = slice(plane * deep, (plane + 1) * deep)
        mine = picked[0, :, :, cols].reshape(SUB * cap, deep)
        both = dot(mine, hid_grads[...], 0, 0)
        backs[plane, 0, 0] = both[:, :FF].astype(BF)
        backs[plane, 0, 1] = both[:, FF:].astype(BF)
        mine = slot_grad[0, :, :, cols].reshape(SUB * cap, deep)
        backs[plane, 0, 2] = dot(mine, acts[...], 0, 0).astype(BF)


def run_experts(first, picked, slot_grads, shards):
    planes, count, _, deep, _ = shards.shape
    cap, width = picked.shape[2:]
    slots = SUB * cap
    rows = pl.BlockSpec((1, SUB, cap, width), lambda e: (first + e, 0, 0, 0))
    out_rows = pl.BlockSpec((1, SUB, cap, width), lambda e: (e, 0, 0, 0))
    block = pl.BlockSpec((planes, 1, 3, deep, FF), lambda e: (0, e, 0, 0, 0))
    return pl.pallas_call(
        expert_kernel,
        grid=(count,),
        in_specs=[rows, rows, block],
        out_specs=[out_rows, out_rows, block],
        out_shape=[jax.ShapeDtypeStruct((count, SUB, cap, width), BF)] * 2
        + [jax.ShapeDtypeStruct(shards.shape, BF)],
        scratch_shapes=[pltpu.VMEM((slots, FF), BF), pltpu.VMEM((slots, 2 * FF), BF)],
        compiler_params=params("arbitrary"),
        cost_estimate=cost(
            18 * count * slots * width * FF, count * (8 * slots * width + 12 * width * FF)
        ),
        name="experts",
    )(picked, slot_grads, shards)


def place_kernel(first, experts, at_ref, *refs):
    pieces, outs, held, sems = refs[:SUB], refs[-5:-2], refs[-2], refs[-1]
    count = pieces[0].shape[0]
    copies = []
    for k in range(SUB):
        owner = lax.bitwise_xor(at_ref[0], k)
        for e in range(count):
            column = pl.multiple_of((owner * experts + (first + e)) * FF, FF)
            for which, out in enumerate(outs):
                at = len(copies)
                held[at] = pieces[k][e, which].astype(F32)
                copy = pltpu.make_async_copy(
                    held.at[at], out.at[:, pl.ds(column, FF)], sems.at[at]
                )
                copy.start()
                copies.append(copy)
    for copy in copies:
        copy.wait()


def place(at, pieces, first, experts, held):
    count, _, rows, _ = pieces[0].shape
    anywhere = pl.BlockSpec(memory_space=pl.ANY)
    in_specs = [pl.BlockSpec(memory_space=pltpu.SMEM)]
    in_specs += [pl.BlockSpec(memory_space=pltpu.VMEM)] * SUB
    held = list(held or ())
    return pl.pallas_call(
        functools.partial(place_kernel, first, experts),
        in_specs=in_specs + [anywhere] * len(held),
        out_specs=[anywhere] * 3,
        out_shape=[jax.ShapeDtypeStruct((rows, SUB * experts * FF), F32)] * 3,
        scratch_shapes=[
            pltpu.VMEM((3 * SUB * count, rows, FF), F32),
            pltpu.SemaphoreType.DMA((3 * SUB * count,)),
        ],
        input_output_aliases={1 + SUB + i: i for i in range(len(held))},
        compiler_params=params(),
        cost_estimate=cost(0, 18 * SUB * count * rows * FF),
        name="place_rows",
    )(at, *pieces, *held)


def norm_scale(values):
    return lax.rsqrt(jnp.mean(values * values, axis=-1, keepdims=True) + EPS)


def norm_backward(values, rms_scale, gain_row, gradient):
    weighted = gradient * gain_row
    centre = jnp.mean(weighted * values, axis=-1, keepdims=True)
    back_values = rms_scale * weighted - values * rms_scale * rms_scale * rms_scale * centre
    return (back_values, jnp.sum(gradient * values * rms_scale, axis=0))


def layer(
    fsdp,
    tp,
    tokens,
    segments,
    slots,
    gate_values,
    gains,
    w_query,
    w_key,
    w_value,
    w_out,
    w_gate,
    w_up,
    w_down,
    cotangent,
):
    length, width = segments.shape[0], tokens.shape[1]
    half = tokens.shape[0]
    planes = fsdp // SUB
    at_fsdp, at_tp = lax.axis_index("fsdp"), lax.axis_index("tp")
    sub, plane = at_fsdp % SUB, at_fsdp // SUB
    at = jnp.stack([sub, plane]).astype(jnp.int32)
    heads_kv = w_key.shape[1] // HEAD_DIM
    group = w_query.shape[1] // w_key.shape[1]
    experts = slots.shape[1] // SUB
    cap = slots.shape[2]

    def swap(values, mask, axis="fsdp"):
        size = fsdp if axis == "fsdp" else tp
        return lax.ppermute(values, axis, [(i, i ^ mask) for i in range(size)])

    def shift(values, planes_on):
        return lax.ppermute(
            values, "fsdp", [(i, (i + planes_on * SUB) % fsdp) for i in range(fsdp)]
        )

    def by_sub(pieces):
        near = [jnp.where((sub & 1) == 1, pieces[k ^ 1], pieces[k]) for k in range(SUB)]
        return [jnp.where((sub & 2) == 2, near[k ^ 2], near[k]) for k in range(SUB)]

    def ordered(mine, other):
        return jnp.where(
            at_tp == 0, jnp.concatenate([mine, other]), jnp.concatenate([other, mine])
        )

    def sequence_gather(mine):
        if tp == 2:
            return ordered(mine, swap(mine, 1, "tp"))
        return lax.all_gather(mine, "tp", axis=0, tiled=True)

    def part_of(values, which):
        return lax.dynamic_slice_in_dim(values, which * half, half, 0)

    def sequence_scatter(values):
        if tp == 2:
            other = swap(part_of(values, 1 - at_tp).astype(BF), 1, "tp")
            return part_of(values, at_tp) + other.astype(F32)
        return lax.psum_scatter(values, "tp", scatter_dimension=0, tiled=True)

    turn = half * at_tp if tp == 2 else 0

    def plane_start(mine):
        if tp == 2:
            return swap(mine, 1, "tp"), swap(mine, 2)
        return (lax.all_gather(mine, "tp", axis=0, tiled=True),)

    def plane_finish(mine, begun):
        if tp == 2:
            beside, across = begun
            cut = half // 2
            corner = (swap(beside[:cut], 2), swap(across[cut:], 1, "tp"))
            first, third = (mine, beside), (across, *corner)
        else:
            first = begun
            third = (swap(first[0], 2),)
        return [first, [swap(p, 1) for p in first], third, [swap(p, 1) for p in third]]

    def plane_scatter(put_one):
        fourth, second = swap(put_one(3, 0, length), 1), swap(put_one(1, 0, length), 1)
        if tp == 2:
            cut = half // 2
            upper = swap(put_one(2, half, cut, (fourth,)), 2)
            lower = swap(put_one(2, half + cut, cut, (fourth,)), 1, "tp")
            across = swap(put_one(2, 0, cut, (fourth,)), 2)
            beside = swap(put_one(0, half + cut, cut, (second,)), 1, "tp")
            across_on = put_one(2, cut, cut, (fourth,), F32)
            beside_on = put_one(0, half, cut, (second,), F32)
            mine = put_one(0, 0, half, (second,), F32)

            def finish(got):
                upper, lower, across, beside = got
                beside_up = swap((beside_on + upper.astype(F32)).astype(BF), 1, "tp")
                across_low = swap((across_on + lower.astype(F32)).astype(BF), 2)
                over_y = jnp.concatenate([across, across_low]).astype(F32)
                over_tp = jnp.concatenate([beside_up, beside]).astype(F32)
                return mine + over_y + over_tp

            return (upper, lower, across, beside), mine, finish
        third = put_one(2, 0, length, (fourth,))
        first = put_one(0, 0, length, (second,), F32)

        def finish(got):
            total = first + got.astype(F32)
            return lax.psum_scatter(total, "tp", scatter_dimension=0, tiled=True)

        return swap(third, 2), third, finish

    def weight_scatter(values):
        values = values.reshape(planes, 2, 2, -1, values.shape[1])
        core, line = sub & 1, sub >> 1
        sent = lax.dynamic_index_in_dim(values, 1 - core, 2, keepdims=False)
        kept = lax.dynamic_index_in_dim(values, core, 2, keepdims=False)
        values = halved = kept.astype(F32) + swap(sent.astype(BF), 1).astype(F32)
        sent = lax.dynamic_index_in_dim(values, 1 - line, 1, keepdims=False)
        kept = lax.dynamic_index_in_dim(values, line, 1, keepdims=False)
        values = kept + swap(sent.astype(BF), 2).astype(F32)

        total = lax.dynamic_index_in_dim(values, plane, 0, keepdims=False)
        got = [
            shift(
                lax.dynamic_index_in_dim(
                    values, (plane + r) % planes, 0, keepdims=False
                ).astype(BF),
                r,
            )
            for r in range(1, planes)
        ]
        return halved, values, got, lambda got: sum([total] + [part.astype(F32) for part in got])

    def gain_scatter(values):
        values = values.reshape(2, planes, SUB, tp, -1)

        def block(which, axis):
            return lax.dynamic_index_in_dim(values, which, axis, keepdims=False)

        if tp == 2:
            values = block(at_tp, 3) + swap(block(1 - at_tp, 3), 1, "tp")
        else:
            values = lax.psum_scatter(values, "tp", scatter_dimension=3)
        values = sum([block(sub, 2)] + [swap(block(sub ^ k, 2), k) for k in range(1, SUB)])
        total = lax.dynamic_index_in_dim(values, plane, 1, keepdims=False)
        got = [
            shift(lax.dynamic_index_in_dim(values, (plane + r) % planes, 1, keepdims=False), r)
            for r in range(1, planes)
        ]
        return values, got, lambda got: sum(got, total)

    across = [[j + SUB * p for p in range(planes)] for j in range(SUB)]
    chunks, taken = [], 0
    for count in CHUNKS:
        count = min(count, experts - taken)
        if count:
            chunks.append((taken, count))
            taken += count

    own_rows = w_gate.shape[0]
    shapes = [(count, 3, own_rows, FF) for _, count in chunks for _ in range(SUB)]

    def cut_plan(at, outs):
        for number, (first, count) in enumerate(chunks):
            for k in (3, 2, 1, 0):
                for e in range(count):
                    column = lax.bitwise_xor(at[0], k) * experts + (first + e)
                    column = pl.multiple_of(column * FF, FF)
                    for which in range(3):
                        out = outs[number * SUB + k]
                        yield which, (slice(None), pl.ds(column, FF)), out, (e, which)

    sends = move(at, (w_gate, w_up, w_down), shapes, 3 * SUB * experts, cut_plan)
    sends = [sends[i : i + SUB] for i in range(0, len(sends), SUB)]

    def swap_all(pieces):
        return [pieces[0]] + [swap(pieces[k], k) for k in range(1, SUB)]

    first_pieces = swap_all(sends[0])

    if tp == 2:
        near_gains = swap(gains, 1, "tp")
        near_gains = jnp.where(
            at_tp == 0,
            jnp.concatenate([gains, near_gains], axis=1),
            jnp.concatenate([near_gains, gains], axis=1),
        )
    else:
        near_gains = lax.all_gather(gains, "tp", axis=1, tiled=True)
    whole_tokens = sequence_gather(tokens)
    near_gains = tie(near_gains, sends[0][1:])
    plane_gains = jnp.concatenate(
        by_sub([near_gains] + [swap(near_gains, k) for k in range(1, SUB)]), axis=1
    )
    all_gains = jnp.stack([plane_gains] + [shift(plane_gains, -r) for r in range(1, planes)])
    all_gains = jnp.concatenate([all_gains, all_gains])
    all_gains = lax.dynamic_slice_in_dim(all_gains, planes - plane, planes, 0)
    all_gains = all_gains.transpose(1, 0, 2).reshape(2, -1)

    rows = w_query.shape[0]
    packed = jnp.concatenate(
        [
            w_query.reshape(rows, heads_kv, group * HEAD_DIM),
            w_key.reshape(rows, heads_kv, HEAD_DIM),
            w_value.reshape(rows, heads_kv, HEAD_DIM),
        ],
        axis=2,
    ).reshape(rows, -1)
    qkv_cols = packed.shape[1]
    attn_w = lax.all_gather(
        jnp.concatenate([packed, w_out], axis=1), "fsdp", axis=0, tiled=True
    )
    qkv_w, out_w = attn_w[:, :qkv_cols], attn_w[:, qkv_cols:]

    live = slots[0] >= 0
    turned = jnp.where(live, (slots[0] + (length - turn)) % length, -1)
    table = jnp.stack([turned.astype(F32), jnp.where(live, gate_values[0], 0.0)])
    table = tie(table, plane_gains)

    def table_for(k):
        return lax.dynamic_slice_in_dim(table, (sub ^ k) * experts, experts, 1)

    tables = [table_for(0)] + [swap(table_for(k), k) for k in range(1, SUB)]

    def shards_of(pieces, others=()):
        count = pieces[0].shape[0]

        def plan(at, outs):
            for k in range(SUB):
                row = pl.multiple_of(lax.bitwise_xor(at[0], k) * own_rows, own_rows)
                taken = (slice(None), slice(None), pl.ds(row, own_rows))
                yield k, (slice(None),), outs[0], taken

        (mine,) = move(at, pieces, [(count, 3, SUB * own_rows, FF)], SUB, plan, others)
        return lax.all_gather(mine, "fsdp", axis_index_groups=across), mine

    held, mine_first = shards_of(first_pieces, (all_gains, whole_tokens))
    shards = [held]

    whole_resid = whole_tokens.astype(F32)
    first_low = (whole_resid * norm_scale(whole_resid) * all_gains[0]).astype(BF)
    begun = plane_start(tie(cotangent, mine_first))
    first_low = tie(first_low, tables)
    qkv = dot(qkv_w, first_low, 0, 1).astype(BF)
    attended, logs = attend(qkv, segments, heads_kv, group)
    attended = tie(attended, begun)
    cots = plane_finish(cotangent, begun)
    resid = tokens.astype(F32)
    attn_part = dot(attended, out_w, 0, 1)
    later = [swap_all(tie(sent, attended)) for sent in sends[1:]]
    if tp == 2:
        got = swap(part_of(attn_part, 1 - at_tp).astype(BF), 1, "tp")
        got = tie(got, cots[2])
        hidden = resid + (part_of(attn_part, at_tp) + got.astype(F32))
    else:
        hidden = resid + sequence_scatter(attn_part)
    scale_two = norm_scale(hidden)
    second_low = (hidden * scale_two * all_gains[1]).astype(BF)

    slot_grads = pick(cots, tables, True)
    begun, later = tie((plane_start(second_low), later), slot_grads)
    shards += [shards_of(pieces)[0] for pieces in later]
    picked = pick(plane_finish(second_low, begun), tables, False)

    sums, slot_outs, pick_grads = [], [], []
    for number, ((first, count), held) in enumerate(zip(chunks, shards)):
        slot_out, pick_grad, backs = run_experts(first, picked, slot_grads, held)
        slot_outs.append(slot_out)
        pick_grads.append(pick_grad)
        sums.append(
            lax.psum_scatter(backs, "fsdp", scatter_dimension=0, axis_index_groups=across)
        )

    got, sent, finish = plane_scatter(
        lambda k, *more: put(pick_grads, tables[k], False, k, *more)
    )
    second_grad = finish(got)
    late_tables = tie(tables, sent)
    got_out, _, finish_out_sum = plane_scatter(
        lambda k, *more: put(slot_outs, late_tables[k], True, k, *more)
    )

    back_two, second_gain = norm_backward(hidden, scale_two, all_gains[1], second_grad)
    grad_hidden = cotangent.astype(F32) + back_two
    own_low = grad_hidden.astype(BF)

    def rows_out(part, others=()):
        part = part.reshape(-1, 3, SUB * rows, FF)

        def plan(at, outs):
            for k in (3, 2, 1, 0):
                row = pl.multiple_of(lax.bitwise_xor(at[0], k) * rows, rows)
                taken = (slice(None), slice(None), pl.ds(row, rows))
                yield 0, taken, outs[k], (slice(None),)

        shapes = [(part.shape[0], 3, rows, FF)] * SUB
        return move(at, (part,), shapes, SUB, plan, others)

    hidden_low = sequence_gather(own_low)
    _, _, got_grad_out, finish_out = weight_scatter(dot(hidden_low, attended, 0, 1))
    attended_grad = dot(out_w, hidden_low, 0, 1).astype(BF)
    qkv_grad = attend_back(qkv, attended_grad, attended, logs, segments, heads_kv, group)
    grad_qkv = dot(first_low, qkv_grad, 0, 1)
    first_part = dot(qkv_grad, qkv_w, 0, 1)
    if tp == 2:
        got = swap(part_of(first_part, 1 - at_tp).astype(BF), 1, "tp")
        first_grad = part_of(first_part, at_tp) + got.astype(F32)
    else:
        first_grad = sequence_scatter(first_part)
    back_one, first_gain = norm_backward(resid, norm_scale(resid), all_gains[0], first_grad)
    grad_tokens = grad_hidden + back_one
    mixed = (hidden + finish_out_sum(tie(got_out, first_gain))).astype(BF)
    grad_gains, got_gains, finish_gains = gain_scatter(jnp.stack([first_gain, second_gain]))
    halved, grad_qkv, got_qkv, finish_qkv = weight_scatter(grad_qkv)

    early = [swap_all(rows_out(part, halved)) for part in sums[:-1]]
    late = rows_out(sums[-1], (grad_qkv, grad_gains, early))
    got_grad_out, got_qkv, got_gains = tie((got_grad_out, got_qkv, got_gains), late[1:])
    late = swap_all(late)
    expert_grads = None
    for number, pieces in enumerate(early):
        expert_grads = place(at, pieces, chunks[number][0], experts, expert_grads)
    expert_grads = place(at, late, chunks[-1][0], experts, expert_grads)
    grad_out = finish_out(got_grad_out)
    grad_gains = finish_gains(got_gains)
    grad_qkv = finish_qkv(got_qkv).reshape(rows, heads_kv, -1)
    cut = group * HEAD_DIM
    return (
        mixed,
        grad_tokens,
        grad_gains,
        grad_qkv[:, :, :cut].reshape(rows, -1),
        grad_qkv[:, :, cut : cut + HEAD_DIM].reshape(rows, -1),
        grad_qkv[:, :, cut + HEAD_DIM :].reshape(rows, -1),
        grad_out,
        *expert_grads,
    )


def solution(mesh):
    both, split = P(("fsdp", "tp"), None), P("fsdp", "tp")
    experts, feature = P("fsdp", "tp", None), P(None, ("fsdp", "tp"))
    return jax.shard_map(
        functools.partial(layer, mesh.shape["fsdp"], mesh.shape["tp"]),
        mesh=mesh,
        in_specs=(both, P("fsdp"), experts, experts, feature) + (split,) * 7 + (both,),
        out_specs=(both, both, feature) + (split,) * 7,
        check_vma=False,
    )
```

```python
import functools

import jax
import jax.numpy as jnp
from jax import lax
from jax.experimental import pallas as pl
from jax.experimental.pallas import tpu as pltpu
from jax.sharding import PartitionSpec as P

HEAD_DIM = 64
FF = 512
EPS = 1e-06
SUB = 4
TILE = 256
NEG = -1e30
LANES = 128
CHUNKS = (3, 1)
VMEM_BYTES = 56 * 1024 * 1024
BF = jnp.bfloat16
F32 = jnp.float32


def params(*semantics):
    return pltpu.CompilerParams(
        vmem_limit_bytes=VMEM_BYTES, dimension_semantics=semantics or None
    )


def cost(flops, moved, exps=0):
    return pl.CostEstimate(flops=int(flops), bytes_accessed=int(moved), transcendentals=int(exps))


def dot(left, right, left_dim=1, right_dim=0):
    return lax.dot_general(
        left, right, (((left_dim,), (right_dim,)), ((), ())), preferred_element_type=F32
    )


def tie_kernel(*refs):
    pass


def tie(values, others):
    leaves, tree = jax.tree.flatten(values)
    others = jax.tree.leaves(others)
    anywhere = pl.BlockSpec(memory_space=pl.ANY)
    outs = pl.pallas_call(
        tie_kernel,
        in_specs=[anywhere] * (len(leaves) + len(others)),
        out_specs=[anywhere] * len(leaves),
        out_shape=[jax.ShapeDtypeStruct(leaf.shape, leaf.dtype) for leaf in leaves],
        input_output_aliases={i: i for i in range(len(leaves))},
        compiler_params=params(),
        cost_estimate=cost(0, 0),
        name="tie",
    )(*leaves, *others)
    return jax.tree.unflatten(tree, outs)


def move_kernel(plan, sources, at_ref, *refs):
    outs, sems = refs[sources:-1], refs[-1]
    copies = [
        pltpu.make_async_copy(refs[i].at[taken], out.at[put_at], sems.at[number])
        for number, (i, taken, out, put_at) in enumerate(plan(at_ref, outs))
    ]
    for copy in copies:
        copy.start()
    for copy in copies:
        copy.wait()


def move(at, sources, shapes, steps, plan, others=()):
    anywhere = pl.BlockSpec(memory_space=pl.ANY)
    operands = [*sources, *jax.tree.leaves(others)]
    return pl.pallas_call(
        functools.partial(move_kernel, plan, len(operands)),
        in_specs=[pl.BlockSpec(memory_space=pltpu.SMEM)] + [anywhere] * len(operands),
        out_specs=[pl.BlockSpec(memory_space=pltpu.VMEM)] * len(shapes),
        out_shape=[jax.ShapeDtypeStruct(shape, BF) for shape in shapes],
        scratch_shapes=[pltpu.SemaphoreType.DMA((steps,))],
        compiler_params=params(),
        cost_estimate=cost(0, 4 * sum(source.size for source in sources)),
        name="move",
    )(at, *operands)


def fill_bias(bias, seg_row, seg_col):
    length = bias.shape[0]

    @pl.when(pl.program_id(0) == 0)
    def _():
        for start in range(0, length, TILE):
            depth = start + TILE
            key_pos = lax.broadcasted_iota(jnp.int32, (depth, TILE), 0)
            query_pos = lax.broadcasted_iota(jnp.int32, (depth, TILE), 1) + start
            allowed = (query_pos >= key_pos) & (
                seg_col[:depth, :] == seg_row[:, start : start + TILE]
            )
            bias[:depth, start : start + TILE] = jnp.where(allowed, 0.0, NEG)


def attend_kernel(group, qkv_ref, seg_row, seg_col, out_ref, log_ref, bias):
    fill_bias(bias, seg_row, seg_col)
    length = bias.shape[0]
    wide = group * HEAD_DIM
    keys = qkv_ref[wide : wide + HEAD_DIM, :].T
    for head in range(group):
        rows = slice(head * HEAD_DIM, (head + 1) * HEAD_DIM)
        for start in range(0, length, TILE):
            depth = start + TILE
            cols = slice(start, depth)
            query = qkv_ref[rows, cols] * jnp.asarray(HEAD_DIM**-0.5, BF)
            scores = dot(keys[:depth], query) + bias[:depth, cols]
            top = jnp.max(scores, axis=0, keepdims=True)
            expo = jnp.exp(scores - top)
            total = jnp.sum(expo, axis=0, keepdims=True)
            mixed = dot(qkv_ref[wide + HEAD_DIM : wide + 2 * HEAD_DIM, :depth], expo.astype(BF))
            out_ref[rows, cols] = (mixed / total).astype(BF)
            log_ref[0, head : head + 1, cols] = top + jnp.log(total)


def attend(qkv, segments, heads_kv, group):
    length = qkv.shape[1]
    wide = (group + 2) * HEAD_DIM
    return pl.pallas_call(
        functools.partial(attend_kernel, group),
        grid=(heads_kv,),
        in_specs=[
            pl.BlockSpec((wide, length), lambda h: (h, 0)),
            pl.BlockSpec((1, length), lambda h: (0, 0)),
            pl.BlockSpec((length, 1), lambda h: (0, 0)),
        ],
        out_specs=[
            pl.BlockSpec((group * HEAD_DIM, length), lambda h: (h, 0)),
            pl.BlockSpec((1, group, length), lambda h: (h, 0, 0)),
        ],
        out_shape=[
            jax.ShapeDtypeStruct((heads_kv * group * HEAD_DIM, length), BF),
            jax.ShapeDtypeStruct((heads_kv, group, length), F32),
        ],
        scratch_shapes=[pltpu.VMEM((length, length), F32)],
        compiler_params=params("arbitrary"),
        cost_estimate=cost(
            heads_kv * group * length * length * HEAD_DIM * 12,
            4 * qkv.size,
            heads_kv * group * length * length,
        ),
        name="attend",
    )(qkv, segments.reshape(1, -1), segments.reshape(-1, 1))


def attend_back_kernel(
    group, qkv_ref, grad_ref, out_ref, log_ref, seg_row, seg_col, back_ref, bias, key_sum, value_sum
):
    fill_bias(bias, seg_row, seg_col)
    length = bias.shape[0]
    wide = group * HEAD_DIM
    scale = HEAD_DIM**-0.5
    keys_t = qkv_ref[wide : wide + HEAD_DIM, :]
    keys = keys_t.T
    values = qkv_ref[wide + HEAD_DIM : wide + 2 * HEAD_DIM, :].T
    key_sum[...] = jnp.zeros_like(key_sum)
    value_sum[...] = jnp.zeros_like(value_sum)
    for head in range(group):
        rows = slice(head * HEAD_DIM, (head + 1) * HEAD_DIM)
        for start in range(0, length, TILE):
            depth = start + TILE
            cols = slice(start, depth)
            query_t = qkv_ref[rows, cols] * jnp.asarray(scale, BF)
            grad_t = grad_ref[rows, cols]
            centre = jnp.sum(
                grad_t.astype(F32) * out_ref[rows, cols].astype(F32), axis=0, keepdims=True
            )
            scores = dot(keys[:depth], query_t) + bias[:depth, cols]
            prob = jnp.exp(scores - log_ref[0, head : head + 1, cols])
            prob_grad = dot(values[:depth], grad_t)
            score_grad = (prob * (prob_grad - centre)).astype(BF)
            back_ref[rows, cols] = (dot(keys_t[:, :depth], score_grad) * scale).astype(BF)
            key_sum[:depth, :] += dot(score_grad, query_t.T)
            value_sum[:depth, :] += dot(prob.astype(BF), grad_t.T)
    back_ref[wide : wide + HEAD_DIM, :] = key_sum[...].T.astype(BF)
    back_ref[wide + HEAD_DIM : wide + 2 * HEAD_DIM, :] = value_sum[...].T.astype(BF)


def attend_back(qkv, grads, attended, logs, segments, heads_kv, group):
    length = qkv.shape[1]
    wide = (group + 2) * HEAD_DIM
    head_block = pl.BlockSpec((group * HEAD_DIM, length), lambda h: (h, 0))
    return pl.pallas_call(
        functools.partial(attend_back_kernel, group),
        grid=(heads_kv,),
        in_specs=[
            pl.BlockSpec((wide, length), lambda h: (h, 0)),
            head_block,
            head_block,
            pl.BlockSpec((1, group, length), lambda h: (h, 0, 0)),
            pl.BlockSpec((1, length), lambda h: (0, 0)),
            pl.BlockSpec((length, 1), lambda h: (0, 0)),
        ],
        out_specs=pl.BlockSpec((wide, length), lambda h: (h, 0)),
        out_shape=jax.ShapeDtypeStruct(qkv.shape, BF),
        scratch_shapes=[
            pltpu.VMEM((length, length), F32),
            pltpu.VMEM((length, HEAD_DIM), F32),
            pltpu.VMEM((length, HEAD_DIM), F32),
        ],
        compiler_params=params("arbitrary"),
        cost_estimate=cost(
            heads_kv * group * length * length * HEAD_DIM * 30,
            8 * qkv.size,
            heads_kv * group * length * length,
        ),
        name="attend_back",
    )(qkv, grads, attended, logs, segments.reshape(1, -1), segments.reshape(-1, 1))


def pick_kernel(weighted, parts, slot_ref, *refs):
    tables, out_ref = refs[:parts], refs[-1]
    cap = out_ref.shape[2]
    expert = pl.program_id(0)

    def column(which):
        row = slot_ref[which, pl.ds(expert, 1), :]
        return jnp.broadcast_to(row, (LANES, cap)).T

    index = column(0)
    lane = lax.broadcasted_iota(jnp.int32, (cap, LANES), 1).astype(F32)
    picked, start = None, 0
    for table in tables:
        marks = [
            (lane + float(start + at) == index).astype(BF)
            for at in range(0, table.shape[0], LANES)
        ]
        part = dot(jnp.concatenate(marks, axis=1), table[...])
        picked = part if picked is None else picked + part
        start += table.shape[0]
    if weighted:
        picked = picked * column(1)[:, :1]
    out_ref[0, 0] = picked.astype(BF)


def pick(tables, slots, weighted):
    _, experts, cap = slots[0].shape
    width = tables[0][0].shape[1]
    held = None
    for k, parts in enumerate(tables):
        args = [slots[k], *parts]
        specs = [pl.BlockSpec(slots[k].shape, lambda e: (0, 0, 0))]
        specs += [pl.BlockSpec(part.shape, lambda e: (0, 0)) for part in parts]
        length = sum(part.shape[0] for part in parts)
        if held is not None:
            args.append(held)
            specs.append(pl.BlockSpec(memory_space=pl.ANY))
        held = pl.pallas_call(
            functools.partial(pick_kernel, weighted, len(parts)),
            grid=(experts,),
            in_specs=specs,
            out_specs=pl.BlockSpec((1, 1, cap, width), lambda e, k=k: (e, k, 0, 0)),
            out_shape=jax.ShapeDtypeStruct((experts, len(tables), cap, width), BF),
            input_output_aliases={} if k == 0 else {len(args) - 1: 0},
            compiler_params=params("arbitrary"),
            cost_estimate=cost(
                2 * experts * cap * length * width, 2 * (length + experts * cap) * width
            ),
            name="pick_rows",
        )(*args)
    return held


def put_kernel(start, weighted, added, slot_ref, *refs):
    parts, out_ref = refs[: len(refs) - 1 - int(added)], refs[-1]
    cap = parts[0].shape[2]
    first = start + pl.program_id(0) * out_ref.shape[0]
    place = (lax.broadcasted_iota(jnp.int32, (out_ref.shape[0], cap), 0) + first).astype(F32)
    total, at = None, 0
    for held in parts:
        for expert in range(held.shape[0]):
            match = place == slot_ref[0, at : at + 1, :]
            if weighted:
                marks = jnp.where(match, slot_ref[1, at : at + 1, :], 0.0).astype(BF)
            else:
                marks = match.astype(BF)
            part = dot(marks, held[expert, 0])
            total = part if total is None else total + part
            at += 1
    if added:
        total = total + refs[-2][...].astype(F32)
    out_ref[...] = total.astype(out_ref.dtype)


def put(parts, slots, weighted, which, start, count, addends=(), kind=BF):
    cap, width = parts[0].shape[2:]
    tile = min(TILE, count)
    in_specs = [pl.BlockSpec(slots.shape, lambda r: (0, 0, 0))]
    in_specs += [
        pl.BlockSpec((p.shape[0], 1, cap, width), lambda r: (0, which, 0, 0)) for p in parts
    ]
    in_specs += [pl.BlockSpec((tile, width), lambda r: (start // tile + r, 0))] * len(addends)
    moved = slots.shape[1] * cap
    return pl.pallas_call(
        functools.partial(put_kernel, start, weighted, bool(addends)),
        grid=(count // tile,),
        in_specs=in_specs,
        out_specs=pl.BlockSpec((tile, width), lambda r: (r, 0)),
        out_shape=jax.ShapeDtypeStruct((count, width), kind),
        compiler_params=params("arbitrary"),
        cost_estimate=cost(2 * moved * count * width, 2 * (count + moved) * width),
        name="put_rows",
    )(slots, *parts, *addends)


def expert_kernel(
    picked, slot_grad, shards, slot_out, pick_grad, backs, acts, hid_grads
):
    cap, width = picked.shape[2:]
    planes, deep = shards.shape[0], shards.shape[3]

    def weights(which):
        return shards[:, 0, which].reshape(width, FF)

    def one(k, carry):
        rows = pl.ds(pl.multiple_of(k * cap, cap), cap)
        gate_pre = dot(picked[0, k], weights(0))
        up_pre = dot(picked[0, k], weights(1))
        sig = 1.0 / (1.0 + jnp.exp(-gate_pre))
        silu = gate_pre * sig
        act = (silu * up_pre).astype(BF)
        acts[rows, :] = act
        slot_out[0, k] = dot(act, weights(2), 1, 1).astype(BF)
        inner = dot(slot_grad[0, k], weights(2))
        gate_grad = (inner * up_pre * sig * (1.0 + gate_pre * (1.0 - sig))).astype(BF)
        up_grad = (inner * silu).astype(BF)
        hid_grads[rows, :FF] = gate_grad
        hid_grads[rows, FF:] = up_grad
        pick_grad[0, k] = (
            dot(gate_grad, weights(0), 1, 1) + dot(up_grad, weights(1), 1, 1)
        ).astype(BF)
        return carry

    lax.fori_loop(0, SUB, one, 0)
    for plane in range(planes):
        cols = slice(plane * deep, (plane + 1) * deep)
        mine = picked[0, :, :, cols].reshape(SUB * cap, deep)
        both = dot(mine, hid_grads[...], 0, 0)
        backs[plane, 0, 0] = both[:, :FF].astype(BF)
        backs[plane, 0, 1] = both[:, FF:].astype(BF)
        mine = slot_grad[0, :, :, cols].reshape(SUB * cap, deep)
        backs[plane, 0, 2] = dot(mine, acts[...], 0, 0).astype(BF)


def run_experts(first, picked, slot_grads, shards):
    planes, count, _, deep, _ = shards.shape
    cap, width = picked.shape[2:]
    slots = SUB * cap
    rows = pl.BlockSpec((1, SUB, cap, width), lambda e: (first + e, 0, 0, 0))
    out_rows = pl.BlockSpec((1, SUB, cap, width), lambda e: (e, 0, 0, 0))
    block = pl.BlockSpec((planes, 1, 3, deep, FF), lambda e: (0, e, 0, 0, 0))
    return pl.pallas_call(
        expert_kernel,
        grid=(count,),
        in_specs=[rows, rows, block],
        out_specs=[out_rows, out_rows, block],
        out_shape=[jax.ShapeDtypeStruct((count, SUB, cap, width), BF)] * 2
        + [jax.ShapeDtypeStruct(shards.shape, BF)],
        scratch_shapes=[pltpu.VMEM((slots, FF), BF), pltpu.VMEM((slots, 2 * FF), BF)],
        compiler_params=params("arbitrary"),
        cost_estimate=cost(
            18 * count * slots * width * FF, count * (8 * slots * width + 12 * width * FF)
        ),
        name="experts",
    )(picked, slot_grads, shards)


def place_kernel(first, experts, at_ref, *refs):
    pieces, outs, held, sems = refs[:SUB], refs[-5:-2], refs[-2], refs[-1]
    count = pieces[0].shape[0]
    copies = []
    for k in range(SUB):
        owner = lax.bitwise_xor(at_ref[0], k)
        for e in range(count):
            column = pl.multiple_of((owner * experts + (first + e)) * FF, FF)
            for which, out in enumerate(outs):
                at = len(copies)
                held[at] = pieces[k][e, which].astype(F32)
                copy = pltpu.make_async_copy(
                    held.at[at], out.at[:, pl.ds(column, FF)], sems.at[at]
                )
                copy.start()
                copies.append(copy)
    for copy in copies:
        copy.wait()


def place(at, pieces, first, experts, held):
    count, _, rows, _ = pieces[0].shape
    anywhere = pl.BlockSpec(memory_space=pl.ANY)
    in_specs = [pl.BlockSpec(memory_space=pltpu.SMEM)]
    in_specs += [pl.BlockSpec(memory_space=pltpu.VMEM)] * SUB
    held = list(held or ())
    return pl.pallas_call(
        functools.partial(place_kernel, first, experts),
        in_specs=in_specs + [anywhere] * len(held),
        out_specs=[anywhere] * 3,
        out_shape=[jax.ShapeDtypeStruct((rows, SUB * experts * FF), F32)] * 3,
        scratch_shapes=[
            pltpu.VMEM((3 * SUB * count, rows, FF), F32),
            pltpu.SemaphoreType.DMA((3 * SUB * count,)),
        ],
        input_output_aliases={1 + SUB + i: i for i in range(len(held))},
        compiler_params=params(),
        cost_estimate=cost(0, 18 * SUB * count * rows * FF),
        name="place_rows",
    )(at, *pieces, *held)


def norm_scale(values):
    return lax.rsqrt(jnp.mean(values * values, axis=-1, keepdims=True) + EPS)


def norm_backward(values, rms_scale, gain_row, gradient):
    weighted = gradient * gain_row
    centre = jnp.mean(weighted * values, axis=-1, keepdims=True)
    back_values = rms_scale * weighted - values * rms_scale * rms_scale * rms_scale * centre
    return (back_values, jnp.sum(gradient * values * rms_scale, axis=0))


def layer(
    fsdp,
    tp,
    tokens,
    segments,
    slots,
    gate_values,
    gains,
    w_query,
    w_key,
    w_value,
    w_out,
    w_gate,
    w_up,
    w_down,
    cotangent,
):
    length, width = segments.shape[0], tokens.shape[1]
    half = tokens.shape[0]
    planes = fsdp // SUB
    at_fsdp, at_tp = lax.axis_index("fsdp"), lax.axis_index("tp")
    sub, plane = at_fsdp % SUB, at_fsdp // SUB
    at = jnp.stack([sub, plane]).astype(jnp.int32)
    heads_kv = w_key.shape[1] // HEAD_DIM
    group = w_query.shape[1] // w_key.shape[1]
    experts = slots.shape[1] // SUB
    cap = slots.shape[2]

    def swap(values, mask, axis="fsdp"):
        size = fsdp if axis == "fsdp" else tp
        return lax.ppermute(values, axis, [(i, i ^ mask) for i in range(size)])

    def shift(values, planes_on):
        return lax.ppermute(
            values, "fsdp", [(i, (i + planes_on * SUB) % fsdp) for i in range(fsdp)]
        )

    def by_sub(pieces):
        near = [jnp.where((sub & 1) == 1, pieces[k ^ 1], pieces[k]) for k in range(SUB)]
        return [jnp.where((sub & 2) == 2, near[k ^ 2], near[k]) for k in range(SUB)]

    def ordered(mine, other):
        return jnp.where(
            at_tp == 0, jnp.concatenate([mine, other]), jnp.concatenate([other, mine])
        )

    def sequence_gather(mine):
        if tp == 2:
            return ordered(mine, swap(mine, 1, "tp"))
        return lax.all_gather(mine, "tp", axis=0, tiled=True)

    def part_of(values, which):
        return lax.dynamic_slice_in_dim(values, which * half, half, 0)

    def sequence_scatter(values):
        if tp == 2:
            other = swap(part_of(values, 1 - at_tp).astype(BF), 1, "tp")
            return part_of(values, at_tp) + other.astype(F32)
        return lax.psum_scatter(values, "tp", scatter_dimension=0, tiled=True)

    turn = half * at_tp if tp == 2 else 0

    def plane_start(mine):
        if tp == 2:
            return swap(mine, 1, "tp"), swap(mine, 2)
        return (lax.all_gather(mine, "tp", axis=0, tiled=True),)

    def plane_finish(mine, begun):
        if tp == 2:
            beside, across = begun
            cut = half // 2
            corner = (swap(beside[:cut], 2), swap(across[cut:], 1, "tp"))
            first, third = (mine, beside), (across, *corner)
        else:
            first = begun
            third = (swap(first[0], 2),)
        return [first, [swap(p, 1) for p in first], third, [swap(p, 1) for p in third]]

    def plane_scatter(put_one):
        fourth, second = swap(put_one(3, 0, length), 1), swap(put_one(1, 0, length), 1)
        if tp == 2:
            cut = half // 2
            upper = swap(put_one(2, half, cut, (fourth,)), 2)
            lower = swap(put_one(2, half + cut, cut, (fourth,)), 1, "tp")
            across = swap(put_one(2, 0, cut, (fourth,)), 2)
            beside = swap(put_one(0, half + cut, cut, (second,)), 1, "tp")
            across_on = put_one(2, cut, cut, (fourth,), F32)
            beside_on = put_one(0, half, cut, (second,), F32)
            mine = put_one(0, 0, half, (second,), F32)

            def finish(got):
                upper, lower, across, beside = got
                beside_up = swap((beside_on + upper.astype(F32)).astype(BF), 1, "tp")
                across_low = swap((across_on + lower.astype(F32)).astype(BF), 2)
                over_y = jnp.concatenate([across, across_low]).astype(F32)
                over_tp = jnp.concatenate([beside_up, beside]).astype(F32)
                return mine + over_y + over_tp

            return (upper, lower, across, beside), mine, finish
        third = put_one(2, 0, length, (fourth,))
        first = put_one(0, 0, length, (second,), F32)

        def finish(got):
            total = first + got.astype(F32)
            return lax.psum_scatter(total, "tp", scatter_dimension=0, tiled=True)

        return swap(third, 2), third, finish

    def weight_scatter(values):
        values = values.reshape(planes, 2, 2, -1, values.shape[1])
        core, line = sub & 1, sub >> 1
        sent = lax.dynamic_index_in_dim(values, 1 - core, 2, keepdims=False)
        kept = lax.dynamic_index_in_dim(values, core, 2, keepdims=False)
        values = halved = kept.astype(F32) + swap(sent.astype(BF), 1).astype(F32)
        sent = lax.dynamic_index_in_dim(values, 1 - line, 1, keepdims=False)
        kept = lax.dynamic_index_in_dim(values, line, 1, keepdims=False)
        values = kept + swap(sent.astype(BF), 2).astype(F32)

        total = lax.dynamic_index_in_dim(values, plane, 0, keepdims=False)
        got = [
            shift(
                lax.dynamic_index_in_dim(
                    values, (plane + r) % planes, 0, keepdims=False
                ).astype(BF),
                r,
            )
            for r in range(1, planes)
        ]
        return halved, values, got, lambda got: sum([total] + [part.astype(F32) for part in got])

    def gain_scatter(values):
        values = values.reshape(2, planes, SUB, tp, -1)

        def block(which, axis):
            return lax.dynamic_index_in_dim(values, which, axis, keepdims=False)

        if tp == 2:
            values = block(at_tp, 3) + swap(block(1 - at_tp, 3), 1, "tp")
        else:
            values = lax.psum_scatter(values, "tp", scatter_dimension=3)
        values = sum([block(sub, 2)] + [swap(block(sub ^ k, 2), k) for k in range(1, SUB)])
        total = lax.dynamic_index_in_dim(values, plane, 1, keepdims=False)
        got = [
            shift(lax.dynamic_index_in_dim(values, (plane + r) % planes, 1, keepdims=False), r)
            for r in range(1, planes)
        ]
        return values, got, lambda got: sum(got, total)

    across = [[j + SUB * p for p in range(planes)] for j in range(SUB)]
    rows = w_query.shape[0]
    packed = jnp.concatenate(
        [
            w_query.reshape(rows, heads_kv, group * HEAD_DIM),
            w_key.reshape(rows, heads_kv, HEAD_DIM),
            w_value.reshape(rows, heads_kv, HEAD_DIM),
        ],
        axis=2,
    ).reshape(rows, -1)
    qkv_cols = packed.shape[1]
    mine_attn = jnp.concatenate([packed, w_out], axis=1)
    line = lax.all_gather(mine_attn, "fsdp", axis_index_groups=across)

    chunks, taken = [], 0
    for count in CHUNKS:
        count = min(count, experts - taken)
        if count:
            chunks.append((taken, count))
            taken += count

    own_rows = w_gate.shape[0]
    shapes = [(count, 3, own_rows, FF) for _, count in chunks for _ in range(SUB)]

    def cut_plan(at, outs):
        for number, (first, count) in enumerate(chunks):
            for k in (3, 2, 1, 0):
                for e in range(count):
                    column = lax.bitwise_xor(at[0], k) * experts + (first + e)
                    column = pl.multiple_of(column * FF, FF)
                    for which in range(3):
                        out = outs[number * SUB + k]
                        yield which, (slice(None), pl.ds(column, FF)), out, (e, which)

    sends = move(at, (w_gate, w_up, w_down), shapes, 3 * SUB * experts, cut_plan)
    sends = [sends[i : i + SUB] for i in range(0, len(sends), SUB)]

    def swap_all(pieces):
        return [pieces[0]] + [swap(pieces[k], k) for k in range(1, SUB)]

    first_pieces = swap_all(sends[0])

    if tp == 2:
        near_gains = swap(gains, 1, "tp")
        near_gains = jnp.where(
            at_tp == 0,
            jnp.concatenate([gains, near_gains], axis=1),
            jnp.concatenate([near_gains, gains], axis=1),
        )
    else:
        near_gains = lax.all_gather(gains, "tp", axis=1, tiled=True)
    whole_tokens = sequence_gather(tokens)
    plane_gains = jnp.concatenate(
        by_sub([near_gains] + [swap(near_gains, k) for k in range(1, SUB)]), axis=1
    )
    all_gains = jnp.stack([plane_gains] + [shift(plane_gains, -r) for r in range(1, planes)])
    all_gains = jnp.concatenate([all_gains, all_gains])
    all_gains = lax.dynamic_slice_in_dim(all_gains, planes - plane, planes, 0)
    all_gains = all_gains.transpose(1, 0, 2).reshape(2, -1)

    live = slots[0] >= 0
    turned = jnp.where(live, (slots[0] + (length - turn)) % length, -1)
    table = jnp.stack([turned.astype(F32), jnp.where(live, gate_values[0], 0.0)])

    def table_for(k):
        return lax.dynamic_slice_in_dim(table, (sub ^ k) * experts, experts, 1)

    tables = [table_for(0)] + [swap(table_for(k), k) for k in range(1, SUB)]

    lines_y = swap(tie(line, plane_gains), 2)
    lines = [line, swap(line, 1), lines_y, swap(lines_y, 1)]
    whole_resid = whole_tokens.astype(F32)
    first_low = (whole_resid * norm_scale(whole_resid) * all_gains[0]).astype(BF)

    def attn_plan(at, outs):
        for k in range(SUB):
            for line in range(planes):
                row = (line * SUB + lax.bitwise_xor(at[0], k)) * rows
                row = pl.multiple_of(row, rows)
                yield k, line, outs[0], (pl.ds(row, rows), slice(None))

    (attn_w,) = move(at, lines, [(fsdp * rows, mine_attn.shape[1])], SUB * planes, attn_plan, first_low)
    qkv_w, out_w = attn_w[:, :qkv_cols], attn_w[:, qkv_cols:]

    def shards_of(pieces, others=()):
        count = pieces[0].shape[0]

        def plan(at, outs):
            for k in range(SUB):
                row = pl.multiple_of(lax.bitwise_xor(at[0], k) * own_rows, own_rows)
                taken = (slice(None), slice(None), pl.ds(row, own_rows))
                yield k, (slice(None),), outs[0], taken

        (mine,) = move(at, pieces, [(count, 3, SUB * own_rows, FF)], SUB, plan, others)
        return lax.all_gather(mine, "fsdp", axis_index_groups=across), mine

    held, mine_first = shards_of(
        first_pieces, (line, near_gains, tables, whole_tokens)
    )
    shards = [held]

    begun = plane_start(tie(cotangent, mine_first))
    first_low = tie(first_low, tables)
    qkv = dot(qkv_w, first_low, 0, 1).astype(BF)
    attended, logs = attend(qkv, segments, heads_kv, group)
    attended = tie(attended, begun)
    cots = plane_finish(cotangent, begun)
    resid = tokens.astype(F32)
    attn_part = dot(attended, out_w, 0, 1)
    later = [swap_all(tie(sent, attended)) for sent in sends[1:]]
    if tp == 2:
        got = swap(part_of(attn_part, 1 - at_tp).astype(BF), 1, "tp")
        got = tie(got, cots[2])
        hidden = resid + (part_of(attn_part, at_tp) + got.astype(F32))
    else:
        hidden = resid + sequence_scatter(attn_part)
    scale_two = norm_scale(hidden)
    second_low = (hidden * scale_two * all_gains[1]).astype(BF)

    slot_grads = pick(cots, tables, True)
    begun, later = tie((plane_start(second_low), later), slot_grads)
    shards += [shards_of(pieces)[0] for pieces in later]
    picked = pick(plane_finish(second_low, begun), tables, False)

    sums, slot_outs, pick_grads = [], [], []
    for number, ((first, count), held) in enumerate(zip(chunks, shards)):
        slot_out, pick_grad, backs = run_experts(first, picked, slot_grads, held)
        slot_outs.append(slot_out)
        pick_grads.append(pick_grad)
        sums.append(
            lax.psum_scatter(backs, "fsdp", scatter_dimension=0, axis_index_groups=across)
        )

    got, sent, finish = plane_scatter(
        lambda k, *more: put(pick_grads, tables[k], False, k, *more)
    )
    second_grad = finish(got)
    late_tables = tie(tables, sent)
    got_out, _, finish_out_sum = plane_scatter(
        lambda k, *more: put(slot_outs, late_tables[k], True, k, *more)
    )

    back_two, second_gain = norm_backward(hidden, scale_two, all_gains[1], second_grad)
    grad_hidden = cotangent.astype(F32) + back_two
    own_low = grad_hidden.astype(BF)

    def rows_out(part, others=()):
        part = part.reshape(-1, 3, SUB * rows, FF)

        def plan(at, outs):
            for k in (3, 2, 1, 0):
                row = pl.multiple_of(lax.bitwise_xor(at[0], k) * rows, rows)
                taken = (slice(None), slice(None), pl.ds(row, rows))
                yield 0, taken, outs[k], (slice(None),)

        shapes = [(part.shape[0], 3, rows, FF)] * SUB
        return move(at, (part,), shapes, SUB, plan, others)

    hidden_low = sequence_gather(own_low)
    _, _, got_grad_out, finish_out = weight_scatter(dot(hidden_low, attended, 0, 1))
    attended_grad = dot(out_w, hidden_low, 0, 1).astype(BF)
    qkv_grad = attend_back(qkv, attended_grad, attended, logs, segments, heads_kv, group)
    grad_qkv = dot(first_low, qkv_grad, 0, 1)
    first_part = dot(qkv_grad, qkv_w, 0, 1)
    if tp == 2:
        got = swap(part_of(first_part, 1 - at_tp).astype(BF), 1, "tp")
        first_grad = part_of(first_part, at_tp) + got.astype(F32)
    else:
        first_grad = sequence_scatter(first_part)
    back_one, first_gain = norm_backward(resid, norm_scale(resid), all_gains[0], first_grad)
    grad_tokens = grad_hidden + back_one
    mixed = (hidden + finish_out_sum(tie(got_out, first_gain))).astype(BF)
    grad_gains, got_gains, finish_gains = gain_scatter(jnp.stack([first_gain, second_gain]))
    halved, grad_qkv, got_qkv, finish_qkv = weight_scatter(grad_qkv)

    early = [swap_all(rows_out(part, halved)) for part in sums[:-1]]
    late = rows_out(sums[-1], (grad_qkv, grad_gains, early))
    got_grad_out, got_qkv, got_gains = tie((got_grad_out, got_qkv, got_gains), late[1:])
    late = swap_all(late)
    expert_grads = None
    for number, pieces in enumerate(early):
        expert_grads = place(at, pieces, chunks[number][0], experts, expert_grads)
    expert_grads = place(at, late, chunks[-1][0], experts, expert_grads)
    grad_out = finish_out(got_grad_out)
    grad_gains = finish_gains(got_gains)
    grad_qkv = finish_qkv(got_qkv).reshape(rows, heads_kv, -1)
    cut = group * HEAD_DIM
    return (
        mixed,
        grad_tokens,
        grad_gains,
        grad_qkv[:, :, :cut].reshape(rows, -1),
        grad_qkv[:, :, cut : cut + HEAD_DIM].reshape(rows, -1),
        grad_qkv[:, :, cut + HEAD_DIM :].reshape(rows, -1),
        grad_out,
        *expert_grads,
    )


def solution(mesh):
    both, split = P(("fsdp", "tp"), None), P("fsdp", "tp")
    experts, feature = P("fsdp", "tp", None), P(None, ("fsdp", "tp"))
    return jax.shard_map(
        functools.partial(layer, mesh.shape["fsdp"], mesh.shape["tp"]),
        mesh=mesh,
        in_specs=(both, P("fsdp"), experts, experts, feature) + (split,) * 7 + (both,),
        out_specs=(both, both, feature) + (split,) * 7,
        check_vma=False,
    )
```

```python
import functools

import jax
import jax.numpy as jnp
from jax import lax
from jax.experimental import pallas as pl
from jax.experimental.pallas import tpu as pltpu
from jax.sharding import PartitionSpec as P

HEAD_DIM = 64
FF = 512
EPS = 1e-06
SUB = 4
TILE = 256
NEG = -1e30
LANES = 128
CHUNKS = (3, 1)
VMEM_BYTES = 56 * 1024 * 1024
BF = jnp.bfloat16
F32 = jnp.float32


def params(*semantics):
    return pltpu.CompilerParams(
        vmem_limit_bytes=VMEM_BYTES, dimension_semantics=semantics or None
    )


def cost(flops, moved, exps=0):
    return pl.CostEstimate(flops=int(flops), bytes_accessed=int(moved), transcendentals=int(exps))


def dot(left, right, left_dim=1, right_dim=0):
    return lax.dot_general(
        left, right, (((left_dim,), (right_dim,)), ((), ())), preferred_element_type=F32
    )


def tie_kernel(*refs):
    pass


def tie(values, others):
    leaves, tree = jax.tree.flatten(values)
    others = jax.tree.leaves(others)
    anywhere = pl.BlockSpec(memory_space=pl.ANY)
    outs = pl.pallas_call(
        tie_kernel,
        in_specs=[anywhere] * (len(leaves) + len(others)),
        out_specs=[anywhere] * len(leaves),
        out_shape=[jax.ShapeDtypeStruct(leaf.shape, leaf.dtype) for leaf in leaves],
        input_output_aliases={i: i for i in range(len(leaves))},
        compiler_params=params(),
        cost_estimate=cost(0, 0),
        name="tie",
    )(*leaves, *others)
    return jax.tree.unflatten(tree, outs)


def move_kernel(plan, sources, at_ref, *refs):
    outs, sems = refs[sources:-1], refs[-1]
    copies = [
        pltpu.make_async_copy(refs[i].at[taken], out.at[put_at], sems.at[number])
        for number, (i, taken, out, put_at) in enumerate(plan(at_ref, outs))
    ]
    for copy in copies:
        copy.start()
    for copy in copies:
        copy.wait()


def move(at, sources, shapes, steps, plan, others=()):
    anywhere = pl.BlockSpec(memory_space=pl.ANY)
    operands = [*sources, *jax.tree.leaves(others)]
    return pl.pallas_call(
        functools.partial(move_kernel, plan, len(operands)),
        in_specs=[pl.BlockSpec(memory_space=pltpu.SMEM)] + [anywhere] * len(operands),
        out_specs=[pl.BlockSpec(memory_space=pltpu.VMEM)] * len(shapes),
        out_shape=[jax.ShapeDtypeStruct(shape, BF) for shape in shapes],
        scratch_shapes=[pltpu.SemaphoreType.DMA((steps,))],
        compiler_params=params(),
        cost_estimate=cost(0, 4 * sum(source.size for source in sources)),
        name="move",
    )(at, *operands)


def fill_bias(bias, seg_row, seg_col):
    length = bias.shape[0]

    @pl.when(pl.program_id(0) == 0)
    def _():
        for start in range(0, length, TILE):
            depth = start + TILE
            key_pos = lax.broadcasted_iota(jnp.int32, (depth, TILE), 0)
            query_pos = lax.broadcasted_iota(jnp.int32, (depth, TILE), 1) + start
            allowed = (query_pos >= key_pos) & (
                seg_col[:depth, :] == seg_row[:, start : start + TILE]
            )
            bias[:depth, start : start + TILE] = jnp.where(allowed, 0.0, NEG)


def attend_kernel(group, qkv_ref, seg_row, seg_col, out_ref, log_ref, bias):
    fill_bias(bias, seg_row, seg_col)
    length = bias.shape[0]
    wide = group * HEAD_DIM
    keys = qkv_ref[wide : wide + HEAD_DIM, :].T
    for head in range(group):
        rows = slice(head * HEAD_DIM, (head + 1) * HEAD_DIM)
        for start in range(0, length, TILE):
            depth = start + TILE
            cols = slice(start, depth)
            query = qkv_ref[rows, cols] * jnp.asarray(HEAD_DIM**-0.5, BF)
            scores = dot(keys[:depth], query) + bias[:depth, cols]
            top = jnp.max(scores, axis=0, keepdims=True)
            expo = jnp.exp(scores - top)
            total = jnp.sum(expo, axis=0, keepdims=True)
            mixed = dot(qkv_ref[wide + HEAD_DIM : wide + 2 * HEAD_DIM, :depth], expo.astype(BF))
            out_ref[rows, cols] = (mixed / total).astype(BF)
            log_ref[0, head : head + 1, cols] = top + jnp.log(total)


def attend(qkv, segments, heads_kv, group):
    length = qkv.shape[1]
    wide = (group + 2) * HEAD_DIM
    return pl.pallas_call(
        functools.partial(attend_kernel, group),
        grid=(heads_kv,),
        in_specs=[
            pl.BlockSpec((wide, length), lambda h: (h, 0)),
            pl.BlockSpec((1, length), lambda h: (0, 0)),
            pl.BlockSpec((length, 1), lambda h: (0, 0)),
        ],
        out_specs=[
            pl.BlockSpec((group * HEAD_DIM, length), lambda h: (h, 0)),
            pl.BlockSpec((1, group, length), lambda h: (h, 0, 0)),
        ],
        out_shape=[
            jax.ShapeDtypeStruct((heads_kv * group * HEAD_DIM, length), BF),
            jax.ShapeDtypeStruct((heads_kv, group, length), F32),
        ],
        scratch_shapes=[pltpu.VMEM((length, length), F32)],
        compiler_params=params("arbitrary"),
        cost_estimate=cost(
            heads_kv * group * length * length * HEAD_DIM * 12,
            4 * qkv.size,
            heads_kv * group * length * length,
        ),
        name="attend",
    )(qkv, segments.reshape(1, -1), segments.reshape(-1, 1))


def attend_back_kernel(
    group, qkv_ref, grad_ref, out_ref, log_ref, seg_row, seg_col, back_ref, bias, key_sum, value_sum
):
    fill_bias(bias, seg_row, seg_col)
    length = bias.shape[0]
    wide = group * HEAD_DIM
    scale = HEAD_DIM**-0.5
    keys_t = qkv_ref[wide : wide + HEAD_DIM, :]
    keys = keys_t.T
    values = qkv_ref[wide + HEAD_DIM : wide + 2 * HEAD_DIM, :].T
    key_sum[...] = jnp.zeros_like(key_sum)
    value_sum[...] = jnp.zeros_like(value_sum)
    for head in range(group):
        rows = slice(head * HEAD_DIM, (head + 1) * HEAD_DIM)
        for start in range(0, length, TILE):
            depth = start + TILE
            cols = slice(start, depth)
            query_t = qkv_ref[rows, cols] * jnp.asarray(scale, BF)
            grad_t = grad_ref[rows, cols]
            centre = jnp.sum(
                grad_t.astype(F32) * out_ref[rows, cols].astype(F32), axis=0, keepdims=True
            )
            scores = dot(keys[:depth], query_t) + bias[:depth, cols]
            prob = jnp.exp(scores - log_ref[0, head : head + 1, cols])
            prob_grad = dot(values[:depth], grad_t)
            score_grad = (prob * (prob_grad - centre)).astype(BF)
            back_ref[rows, cols] = (dot(keys_t[:, :depth], score_grad) * scale).astype(BF)
            key_sum[:depth, :] += dot(score_grad, query_t.T)
            value_sum[:depth, :] += dot(prob.astype(BF), grad_t.T)
    back_ref[wide : wide + HEAD_DIM, :] = key_sum[...].T.astype(BF)
    back_ref[wide + HEAD_DIM : wide + 2 * HEAD_DIM, :] = value_sum[...].T.astype(BF)


def attend_back(qkv, grads, attended, logs, segments, heads_kv, group):
    length = qkv.shape[1]
    wide = (group + 2) * HEAD_DIM
    head_block = pl.BlockSpec((group * HEAD_DIM, length), lambda h: (h, 0))
    return pl.pallas_call(
        functools.partial(attend_back_kernel, group),
        grid=(heads_kv,),
        in_specs=[
            pl.BlockSpec((wide, length), lambda h: (h, 0)),
            head_block,
            head_block,
            pl.BlockSpec((1, group, length), lambda h: (h, 0, 0)),
            pl.BlockSpec((1, length), lambda h: (0, 0)),
            pl.BlockSpec((length, 1), lambda h: (0, 0)),
        ],
        out_specs=pl.BlockSpec((wide, length), lambda h: (h, 0)),
        out_shape=jax.ShapeDtypeStruct(qkv.shape, BF),
        scratch_shapes=[
            pltpu.VMEM((length, length), F32),
            pltpu.VMEM((length, HEAD_DIM), F32),
            pltpu.VMEM((length, HEAD_DIM), F32),
        ],
        compiler_params=params("arbitrary"),
        cost_estimate=cost(
            heads_kv * group * length * length * HEAD_DIM * 30,
            8 * qkv.size,
            heads_kv * group * length * length,
        ),
        name="attend_back",
    )(qkv, grads, attended, logs, segments.reshape(1, -1), segments.reshape(-1, 1))


def pick_kernel(weighted, parts, slot_ref, *refs):
    tables, out_ref = refs[:parts], refs[-1]
    cap = out_ref.shape[2]
    expert = pl.program_id(0)

    def column(which):
        row = slot_ref[which, pl.ds(expert, 1), :]
        return jnp.broadcast_to(row, (LANES, cap)).T

    index = column(0)
    lane = lax.broadcasted_iota(jnp.int32, (cap, LANES), 1).astype(F32)
    picked, start = None, 0
    for table in tables:
        marks = [
            (lane + float(start + at) == index).astype(BF)
            for at in range(0, table.shape[0], LANES)
        ]
        part = dot(jnp.concatenate(marks, axis=1), table[...])
        picked = part if picked is None else picked + part
        start += table.shape[0]
    if weighted:
        picked = picked * column(1)[:, :1]
    out_ref[0, 0] = picked.astype(BF)


def pick(tables, slots, weighted):
    _, experts, cap = slots[0].shape
    width = tables[0][0].shape[1]
    held = None
    for k, parts in enumerate(tables):
        args = [slots[k], *parts]
        specs = [pl.BlockSpec(slots[k].shape, lambda e: (0, 0, 0))]
        specs += [pl.BlockSpec(part.shape, lambda e: (0, 0)) for part in parts]
        length = sum(part.shape[0] for part in parts)
        if held is not None:
            args.append(held)
            specs.append(pl.BlockSpec(memory_space=pl.ANY))
        held = pl.pallas_call(
            functools.partial(pick_kernel, weighted, len(parts)),
            grid=(experts,),
            in_specs=specs,
            out_specs=pl.BlockSpec((1, 1, cap, width), lambda e, k=k: (e, k, 0, 0)),
            out_shape=jax.ShapeDtypeStruct((experts, len(tables), cap, width), BF),
            input_output_aliases={} if k == 0 else {len(args) - 1: 0},
            compiler_params=params("arbitrary"),
            cost_estimate=cost(
                2 * experts * cap * length * width, 2 * (length + experts * cap) * width
            ),
            name="pick_rows",
        )(*args)
    return held


def put_kernel(start, weighted, added, slot_ref, *refs):
    parts, out_ref = refs[: len(refs) - 1 - int(added)], refs[-1]
    cap = parts[0].shape[2]
    first = start + pl.program_id(0) * out_ref.shape[0]
    place = (lax.broadcasted_iota(jnp.int32, (out_ref.shape[0], cap), 0) + first).astype(F32)
    total, at = None, 0
    for held in parts:
        for expert in range(held.shape[0]):
            match = place == slot_ref[0, at : at + 1, :]
            if weighted:
                marks = jnp.where(match, slot_ref[1, at : at + 1, :], 0.0).astype(BF)
            else:
                marks = match.astype(BF)
            part = dot(marks, held[expert, 0])
            total = part if total is None else total + part
            at += 1
    if added:
        total = total + refs[-2][...].astype(F32)
    out_ref[...] = total.astype(out_ref.dtype)


def put(parts, slots, weighted, which, start, count, addends=(), kind=BF):
    cap, width = parts[0].shape[2:]
    tile = min(TILE, count)
    in_specs = [pl.BlockSpec(slots.shape, lambda r: (0, 0, 0))]
    in_specs += [
        pl.BlockSpec((p.shape[0], 1, cap, width), lambda r: (0, which, 0, 0)) for p in parts
    ]
    in_specs += [pl.BlockSpec((tile, width), lambda r: (start // tile + r, 0))] * len(addends)
    moved = slots.shape[1] * cap
    return pl.pallas_call(
        functools.partial(put_kernel, start, weighted, bool(addends)),
        grid=(count // tile,),
        in_specs=in_specs,
        out_specs=pl.BlockSpec((tile, width), lambda r: (r, 0)),
        out_shape=jax.ShapeDtypeStruct((count, width), kind),
        compiler_params=params("arbitrary"),
        cost_estimate=cost(2 * moved * count * width, 2 * (count + moved) * width),
        name="put_rows",
    )(slots, *parts, *addends)


def expert_kernel(
    picked, slot_grad, shards, slot_out, pick_grad, backs, acts, hid_grads
):
    cap, width = picked.shape[2:]
    planes, deep = shards.shape[0], shards.shape[3]

    def weights(which):
        return shards[:, 0, which].reshape(width, FF)

    def one(k, carry):
        rows = pl.ds(pl.multiple_of(k * cap, cap), cap)
        gate_pre = dot(picked[0, k], weights(0))
        up_pre = dot(picked[0, k], weights(1))
        sig = 1.0 / (1.0 + jnp.exp(-gate_pre))
        silu = gate_pre * sig
        act = (silu * up_pre).astype(BF)
        acts[rows, :] = act
        slot_out[0, k] = dot(act, weights(2), 1, 1).astype(BF)
        inner = dot(slot_grad[0, k], weights(2))
        gate_grad = (inner * up_pre * sig * (1.0 + gate_pre * (1.0 - sig))).astype(BF)
        up_grad = (inner * silu).astype(BF)
        hid_grads[rows, :FF] = gate_grad
        hid_grads[rows, FF:] = up_grad
        pick_grad[0, k] = (
            dot(gate_grad, weights(0), 1, 1) + dot(up_grad, weights(1), 1, 1)
        ).astype(BF)
        return carry

    lax.fori_loop(0, SUB, one, 0)
    for plane in range(planes):
        cols = slice(plane * deep, (plane + 1) * deep)
        mine = picked[0, :, :, cols].reshape(SUB * cap, deep)
        both = dot(mine, hid_grads[...], 0, 0)
        backs[plane, 0, 0] = both[:, :FF].astype(BF)
        backs[plane, 0, 1] = both[:, FF:].astype(BF)
        mine = slot_grad[0, :, :, cols].reshape(SUB * cap, deep)
        backs[plane, 0, 2] = dot(mine, acts[...], 0, 0).astype(BF)


def run_experts(first, picked, slot_grads, shards):
    planes, count, _, deep, _ = shards.shape
    cap, width = picked.shape[2:]
    slots = SUB * cap
    rows = pl.BlockSpec((1, SUB, cap, width), lambda e: (first + e, 0, 0, 0))
    out_rows = pl.BlockSpec((1, SUB, cap, width), lambda e: (e, 0, 0, 0))
    block = pl.BlockSpec((planes, 1, 3, deep, FF), lambda e: (0, e, 0, 0, 0))
    return pl.pallas_call(
        expert_kernel,
        grid=(count,),
        in_specs=[rows, rows, block],
        out_specs=[out_rows, out_rows, block],
        out_shape=[jax.ShapeDtypeStruct((count, SUB, cap, width), BF)] * 2
        + [jax.ShapeDtypeStruct(shards.shape, BF)],
        scratch_shapes=[pltpu.VMEM((slots, FF), BF), pltpu.VMEM((slots, 2 * FF), BF)],
        compiler_params=params("arbitrary"),
        cost_estimate=cost(
            18 * count * slots * width * FF, count * (8 * slots * width + 12 * width * FF)
        ),
        name="experts",
    )(picked, slot_grads, shards)


def place_kernel(first, experts, at_ref, *refs):
    pieces, outs, held, sems = refs[:SUB], refs[-5:-2], refs[-2], refs[-1]
    count = pieces[0].shape[0]
    copies = []
    for k in range(SUB):
        owner = lax.bitwise_xor(at_ref[0], k)
        for e in range(count):
            column = pl.multiple_of((owner * experts + (first + e)) * FF, FF)
            for which, out in enumerate(outs):
                at = len(copies)
                held[at] = pieces[k][e, which].astype(F32)
                copy = pltpu.make_async_copy(
                    held.at[at], out.at[:, pl.ds(column, FF)], sems.at[at]
                )
                copy.start()
                copies.append(copy)
    for copy in copies:
        copy.wait()


def place(at, pieces, first, experts, held):
    count, _, rows, _ = pieces[0].shape
    anywhere = pl.BlockSpec(memory_space=pl.ANY)
    in_specs = [pl.BlockSpec(memory_space=pltpu.SMEM)]
    in_specs += [pl.BlockSpec(memory_space=pltpu.VMEM)] * SUB
    held = list(held or ())
    return pl.pallas_call(
        functools.partial(place_kernel, first, experts),
        in_specs=in_specs + [anywhere] * len(held),
        out_specs=[anywhere] * 3,
        out_shape=[jax.ShapeDtypeStruct((rows, SUB * experts * FF), F32)] * 3,
        scratch_shapes=[
            pltpu.VMEM((3 * SUB * count, rows, FF), F32),
            pltpu.SemaphoreType.DMA((3 * SUB * count,)),
        ],
        input_output_aliases={1 + SUB + i: i for i in range(len(held))},
        compiler_params=params(),
        cost_estimate=cost(0, 18 * SUB * count * rows * FF),
        name="place_rows",
    )(at, *pieces, *held)


def norm_scale(values):
    return lax.rsqrt(jnp.mean(values * values, axis=-1, keepdims=True) + EPS)


def norm_backward(values, rms_scale, gain_row, gradient):
    weighted = gradient * gain_row
    centre = jnp.mean(weighted * values, axis=-1, keepdims=True)
    back_values = rms_scale * weighted - values * rms_scale * rms_scale * rms_scale * centre
    return (back_values, jnp.sum(gradient * values * rms_scale, axis=0))


def layer(
    fsdp,
    tp,
    tokens,
    segments,
    slots,
    gate_values,
    gains,
    w_query,
    w_key,
    w_value,
    w_out,
    w_gate,
    w_up,
    w_down,
    cotangent,
):
    length, width = segments.shape[0], tokens.shape[1]
    half = tokens.shape[0]
    planes = fsdp // SUB
    at_fsdp, at_tp = lax.axis_index("fsdp"), lax.axis_index("tp")
    sub, plane = at_fsdp % SUB, at_fsdp // SUB
    at = jnp.stack([sub, plane]).astype(jnp.int32)
    heads_kv = w_key.shape[1] // HEAD_DIM
    group = w_query.shape[1] // w_key.shape[1]
    experts = slots.shape[1] // SUB
    cap = slots.shape[2]

    def swap(values, mask, axis="fsdp"):
        size = fsdp if axis == "fsdp" else tp
        return lax.ppermute(values, axis, [(i, i ^ mask) for i in range(size)])

    def shift(values, planes_on):
        return lax.ppermute(
            values, "fsdp", [(i, (i + planes_on * SUB) % fsdp) for i in range(fsdp)]
        )

    def by_sub(pieces):
        near = [jnp.where((sub & 1) == 1, pieces[k ^ 1], pieces[k]) for k in range(SUB)]
        return [jnp.where((sub & 2) == 2, near[k ^ 2], near[k]) for k in range(SUB)]

    def ordered(mine, other):
        return jnp.where(
            at_tp == 0, jnp.concatenate([mine, other]), jnp.concatenate([other, mine])
        )

    def sequence_gather(mine):
        if tp == 2:
            return ordered(mine, swap(mine, 1, "tp"))
        return lax.all_gather(mine, "tp", axis=0, tiled=True)

    def part_of(values, which):
        return lax.dynamic_slice_in_dim(values, which * half, half, 0)

    def sequence_scatter(values):
        if tp == 2:
            other = swap(part_of(values, 1 - at_tp).astype(BF), 1, "tp")
            return part_of(values, at_tp) + other.astype(F32)
        return lax.psum_scatter(values, "tp", scatter_dimension=0, tiled=True)

    turn = half * at_tp if tp == 2 else 0

    def plane_start(mine):
        if tp == 2:
            return swap(mine, 1, "tp"), swap(mine, 2)
        return (lax.all_gather(mine, "tp", axis=0, tiled=True),)

    def plane_finish(mine, begun):
        if tp == 2:
            beside, across = begun
            cut = half // 2
            corner = (swap(beside[:cut], 2), swap(across[cut:], 1, "tp"))
            first, third = (mine, beside), (across, *corner)
        else:
            first = begun
            third = (swap(first[0], 2),)
        return [first, [swap(p, 1) for p in first], third, [swap(p, 1) for p in third]]

    def plane_scatter(put_one):
        fourth, second = swap(put_one(3, 0, length), 1), swap(put_one(1, 0, length), 1)
        if tp == 2:
            cut = half // 2
            upper = swap(put_one(2, half, cut, (fourth,)), 2)
            lower = swap(put_one(2, half + cut, cut, (fourth,)), 1, "tp")
            across = swap(put_one(2, 0, cut, (fourth,)), 2)
            beside = swap(put_one(0, half + cut, cut, (second,)), 1, "tp")
            across_on = put_one(2, cut, cut, (fourth,), F32)
            beside_on = put_one(0, half, cut, (second,), F32)
            mine = put_one(0, 0, half, (second,), F32)

            def finish(got):
                upper, lower, across, beside = got
                beside_up = swap((beside_on + upper.astype(F32)).astype(BF), 1, "tp")
                across_low = swap((across_on + lower.astype(F32)).astype(BF), 2)
                over_y = jnp.concatenate([across, across_low]).astype(F32)
                over_tp = jnp.concatenate([beside_up, beside]).astype(F32)
                return mine + over_y + over_tp

            return (upper, lower, across, beside), mine, finish
        third = put_one(2, 0, length, (fourth,))
        first = put_one(0, 0, length, (second,), F32)

        def finish(got):
            total = first + got.astype(F32)
            return lax.psum_scatter(total, "tp", scatter_dimension=0, tiled=True)

        return swap(third, 2), third, finish

    def weight_scatter(values):
        values = values.reshape(planes, 2, 2, -1, values.shape[1])
        core, line = sub & 1, sub >> 1
        sent = lax.dynamic_index_in_dim(values, 1 - core, 2, keepdims=False)
        kept = lax.dynamic_index_in_dim(values, core, 2, keepdims=False)
        values = kept.astype(F32) + swap(sent.astype(BF), 1).astype(F32)
        sent = lax.dynamic_index_in_dim(values, 1 - line, 1, keepdims=False)
        kept = lax.dynamic_index_in_dim(values, line, 1, keepdims=False)
        values = kept + swap(sent.astype(BF), 2).astype(F32)

        total = lax.dynamic_index_in_dim(values, plane, 0, keepdims=False)
        got = [
            shift(
                lax.dynamic_index_in_dim(
                    values, (plane + r) % planes, 0, keepdims=False
                ).astype(BF),
                r,
            )
            for r in range(1, planes)
        ]
        return values, got, lambda got: sum([total] + [part.astype(F32) for part in got])

    def gain_scatter(values):
        values = values.reshape(2, planes, SUB, tp, -1)

        def block(which, axis):
            return lax.dynamic_index_in_dim(values, which, axis, keepdims=False)

        if tp == 2:
            values = block(at_tp, 3) + swap(block(1 - at_tp, 3), 1, "tp")
        else:
            values = lax.psum_scatter(values, "tp", scatter_dimension=3)
        values = sum([block(sub, 2)] + [swap(block(sub ^ k, 2), k) for k in range(1, SUB)])
        total = lax.dynamic_index_in_dim(values, plane, 1, keepdims=False)
        got = [
            shift(lax.dynamic_index_in_dim(values, (plane + r) % planes, 1, keepdims=False), r)
            for r in range(1, planes)
        ]
        return values, got, lambda got: sum(got, total)

    across = [[j + SUB * p for p in range(planes)] for j in range(SUB)]
    rows = w_query.shape[0]
    packed = jnp.concatenate(
        [
            w_query.reshape(rows, heads_kv, group * HEAD_DIM),
            w_key.reshape(rows, heads_kv, HEAD_DIM),
            w_value.reshape(rows, heads_kv, HEAD_DIM),
        ],
        axis=2,
    ).reshape(rows, -1)
    qkv_cols = packed.shape[1]
    mine_attn = jnp.concatenate([packed, w_out], axis=1)
    line = lax.all_gather(mine_attn, "fsdp", axis_index_groups=across)

    chunks, taken = [], 0
    for count in CHUNKS:
        count = min(count, experts - taken)
        if count:
            chunks.append((taken, count))
            taken += count

    own_rows = w_gate.shape[0]
    shapes = [(count, 3, own_rows, FF) for _, count in chunks for _ in range(SUB)]

    def cut_plan(at, outs):
        for number, (first, count) in enumerate(chunks):
            for k in (3, 2, 1, 0):
                for e in range(count):
                    column = lax.bitwise_xor(at[0], k) * experts + (first + e)
                    column = pl.multiple_of(column * FF, FF)
                    for which in range(3):
                        out = outs[number * SUB + k]
                        yield which, (slice(None), pl.ds(column, FF)), out, (e, which)

    sends = move(at, (w_gate, w_up, w_down), shapes, 3 * SUB * experts, cut_plan)
    sends = [sends[i : i + SUB] for i in range(0, len(sends), SUB)]

    def swap_all(pieces):
        return [pieces[0]] + [swap(pieces[k], k) for k in range(1, SUB)]

    first_pieces = swap_all(sends[0])

    if tp == 2:
        near_gains = swap(gains, 1, "tp")
        near_gains = jnp.where(
            at_tp == 0,
            jnp.concatenate([gains, near_gains], axis=1),
            jnp.concatenate([near_gains, gains], axis=1),
        )
    else:
        near_gains = lax.all_gather(gains, "tp", axis=1, tiled=True)
    whole_tokens = sequence_gather(tokens)
    plane_gains = jnp.concatenate(
        by_sub([near_gains] + [swap(near_gains, k) for k in range(1, SUB)]), axis=1
    )
    all_gains = jnp.stack([plane_gains] + [shift(plane_gains, -r) for r in range(1, planes)])
    all_gains = jnp.concatenate([all_gains, all_gains])
    all_gains = lax.dynamic_slice_in_dim(all_gains, planes - plane, planes, 0)
    all_gains = all_gains.transpose(1, 0, 2).reshape(2, -1)

    live = slots[0] >= 0
    turned = jnp.where(live, (slots[0] + (length - turn)) % length, -1)
    table = jnp.stack([turned.astype(F32), jnp.where(live, gate_values[0], 0.0)])

    def table_for(k):
        return lax.dynamic_slice_in_dim(table, (sub ^ k) * experts, experts, 1)

    tables = [table_for(0)] + [swap(table_for(k), k) for k in range(1, SUB)]

    lines_y = swap(tie(line, plane_gains), 2)
    lines = [line, swap(line, 1), lines_y, swap(lines_y, 1)]
    whole_resid = whole_tokens.astype(F32)
    first_low = (whole_resid * norm_scale(whole_resid) * all_gains[0]).astype(BF)

    def attn_plan(at, outs):
        for k in range(SUB):
            for line in range(planes):
                row = (line * SUB + lax.bitwise_xor(at[0], k)) * rows
                row = pl.multiple_of(row, rows)
                yield k, line, outs[0], (pl.ds(row, rows), slice(None))

    (attn_w,) = move(at, lines, [(fsdp * rows, mine_attn.shape[1])], SUB * planes, attn_plan, first_low)
    qkv_w, out_w = attn_w[:, :qkv_cols], attn_w[:, qkv_cols:]

    def shards_of(pieces, others=()):
        count = pieces[0].shape[0]

        def plan(at, outs):
            for k in range(SUB):
                row = pl.multiple_of(lax.bitwise_xor(at[0], k) * own_rows, own_rows)
                taken = (slice(None), slice(None), pl.ds(row, own_rows))
                yield k, (slice(None),), outs[0], taken

        (mine,) = move(at, pieces, [(count, 3, SUB * own_rows, FF)], SUB, plan, others)
        return lax.all_gather(mine, "fsdp", axis_index_groups=across), mine

    held, mine_first = shards_of(
        first_pieces, (line, near_gains, tables, whole_tokens)
    )
    shards = [held]

    begun = plane_start(tie(cotangent, mine_first))
    first_low = tie(first_low, tables)
    qkv = dot(qkv_w, first_low, 0, 1).astype(BF)
    attended, logs = attend(qkv, segments, heads_kv, group)
    attended = tie(attended, begun)
    cots = plane_finish(cotangent, begun)
    resid = tokens.astype(F32)
    attn_part = dot(attended, out_w, 0, 1)
    later = [swap_all(tie(sent, attended)) for sent in sends[1:]]
    if tp == 2:
        got = swap(part_of(attn_part, 1 - at_tp).astype(BF), 1, "tp")
        got = tie(got, cots[2])
        hidden = resid + (part_of(attn_part, at_tp) + got.astype(F32))
    else:
        hidden = resid + sequence_scatter(attn_part)
    scale_two = norm_scale(hidden)
    second_low = (hidden * scale_two * all_gains[1]).astype(BF)

    slot_grads = pick(cots, tables, True)
    begun, later = tie((plane_start(second_low), later), slot_grads)
    shards += [shards_of(pieces)[0] for pieces in later]
    picked = pick(plane_finish(second_low, begun), tables, False)

    sums, slot_outs, pick_grads = [], [], []
    for number, ((first, count), held) in enumerate(zip(chunks, shards)):
        slot_out, pick_grad, backs = run_experts(first, picked, slot_grads, held)
        slot_outs.append(slot_out)
        pick_grads.append(pick_grad)
        sums.append(
            lax.psum_scatter(backs, "fsdp", scatter_dimension=0, axis_index_groups=across)
        )

    got, sent, finish = plane_scatter(
        lambda k, *more: put(pick_grads, tables[k], False, k, *more)
    )
    second_grad = finish(got)
    late_tables = tie(tables, sent)
    got_out, _, finish_out_sum = plane_scatter(
        lambda k, *more: put(slot_outs, late_tables[k], True, k, *more)
    )

    back_two, second_gain = norm_backward(hidden, scale_two, all_gains[1], second_grad)
    grad_hidden = cotangent.astype(F32) + back_two
    own_low = grad_hidden.astype(BF)

    def rows_out(part, others=()):
        part = part.reshape(-1, 3, SUB * rows, FF)

        def plan(at, outs):
            for k in (3, 2, 1, 0):
                row = pl.multiple_of(lax.bitwise_xor(at[0], k) * rows, rows)
                taken = (slice(None), slice(None), pl.ds(row, rows))
                yield 0, taken, outs[k], (slice(None),)

        shapes = [(part.shape[0], 3, rows, FF)] * SUB
        return move(at, (part,), shapes, SUB, plan, others)

    hidden_low = sequence_gather(own_low)
    _, got_grad_out, finish_out = weight_scatter(dot(hidden_low, attended, 0, 1))
    attended_grad = dot(out_w, hidden_low, 0, 1).astype(BF)
    qkv_grad = attend_back(qkv, attended_grad, attended, logs, segments, heads_kv, group)
    grad_qkv = dot(first_low, qkv_grad, 0, 1)
    first_part = dot(qkv_grad, qkv_w, 0, 1)
    early = [rows_out(part, first_part) for part in sums[:-1]]
    if tp == 2:
        got = swap(part_of(first_part, 1 - at_tp).astype(BF), 1, "tp")
        got = tie(got, early)
        first_grad = part_of(first_part, at_tp) + got.astype(F32)
    else:
        first_grad = sequence_scatter(first_part)
    back_one, first_gain = norm_backward(resid, norm_scale(resid), all_gains[0], first_grad)
    grad_tokens = grad_hidden + back_one
    mixed = (hidden + finish_out_sum(tie(got_out, first_gain))).astype(BF)
    grad_gains, got_gains, finish_gains = gain_scatter(jnp.stack([first_gain, second_gain]))
    grad_qkv, got_qkv, finish_qkv = weight_scatter(grad_qkv)

    expert_grads = None
    for number, pieces in enumerate(early):
        pieces = swap_all(tie(pieces, grad_gains))
        expert_grads = place(at, pieces, chunks[number][0], experts, expert_grads)
    late = rows_out(sums[-1], (grad_qkv, grad_gains, expert_grads))
    got_grad_out, got_qkv, got_gains = tie((got_grad_out, got_qkv, got_gains), late[1:])
    late = swap_all(late)
    expert_grads = place(at, late, chunks[-1][0], experts, expert_grads)
    grad_out = finish_out(got_grad_out)
    grad_gains = finish_gains(got_gains)
    grad_qkv = finish_qkv(got_qkv).reshape(rows, heads_kv, -1)
    cut = group * HEAD_DIM
    return (
        mixed,
        grad_tokens,
        grad_gains,
        grad_qkv[:, :, :cut].reshape(rows, -1),
        grad_qkv[:, :, cut : cut + HEAD_DIM].reshape(rows, -1),
        grad_qkv[:, :, cut + HEAD_DIM :].reshape(rows, -1),
        grad_out,
        *expert_grads,
    )


def solution(mesh):
    both, split = P(("fsdp", "tp"), None), P("fsdp", "tp")
    experts, feature = P("fsdp", "tp", None), P(None, ("fsdp", "tp"))
    return jax.shard_map(
        functools.partial(layer, mesh.shape["fsdp"], mesh.shape["tp"]),
        mesh=mesh,
        in_specs=(both, P("fsdp"), experts, experts, feature) + (split,) * 7 + (both,),
        out_specs=(both, both, feature) + (split,) * 7,
        check_vma=False,
    )
```
